256 devices in a mesh: leaf: 64 (over y, x, z_lo), panel: 4 (over z_hi, core).
Axes of the slice: x: 4, y: 4, z: 8 (z_hi: 2, z_lo: 4; z = z_hi * 4 + z_lo), core: 2. Of those that a mesh axis runs over, the one named last changes fastest.
Arguments:
- child_front: bfloat16 [16384, 16384], P('leaf', 'panel'), may hold values from -6 to 6
- own_map: int32 [3, 64, 2], P(None, 'leaf'), may hold values from 0 to 1, each once within a row
- cross_map: int32 [3, 64, 2], P(None, 'leaf'), may hold values from 0 to 1, each once within a row
- pivot_inverse: bfloat16 [7, 512, 512], replicated, may hold values from -0.0029296875 to 0.0029296875
Outputs:
- schur: bfloat16 [16384, 16384], P('leaf', 'panel')
The draws below stay inside these ranges and needn't reach their ends.
Inputs may be any that keep to these rules, and one draw needn't show every extreme that they name: Each own_map[k, d, :] is a permutation of the 2 blocks. Each cross_map[k, d, :] is a permutation of the 2 blocks.
All inputs are finite; a program needn't handle non-finite values.
Results may differ from the reference program's by a relative error of at most 0.0088.
Values may be sent and summed in bfloat16 or wider, within the bound.
A program may use at most 64 MiB of HBM per device.

```python
import jax
import jax.numpy as jnp
from jax import lax

NF = 16384
PANEL = 512
BLOCK = 128
LEVELS = 3
INVERSES = 7
ROWS_DEV = 256
NB = 2
LEAF_BITS = 6
FRONT_ROWS = 16384
N_LEAF = 64


def steps_of(own_key, dims, pieces, low, high):
    loudness, own = 1.0, jax.random.fold_in(own_key, 6)
    for position, blocks in pieces:
        heights = jnp.exp(jax.random.uniform(jax.random.fold_in(own, position), (blocks,), jnp.float32, low / len(pieces), high / len(pieces)))
        loudness = loudness * jnp.repeat(heights, dims[position] // blocks).reshape([-1 if axis == position else 1 for axis in range(len(dims))])
    return loudness


def bell_draw(key, dims, scale, reach, shards=(), kind=jnp.bfloat16):
    factor_of = steps_of(key, dims, shards, -0.22, 0.18) if shards else 1.0
    drawn = jax.random.normal(key, dims, jnp.float32) * scale * factor_of
    return jnp.minimum(jnp.maximum(drawn, -reach), reach).astype(kind)


def setup_inputs(seed: int = 0) -> dict:
    arg_keys = jax.random.split(jax.random.key(seed), 5)
    return {
        "child_front": bell_draw(arg_keys[0], (FRONT_ROWS, NF), 1.0, 6.0, ((0, 64), (1, 4))),
        "own_map": jax.vmap(lambda own: jax.random.permutation(own, NB))(jax.random.split(arg_keys[1], LEVELS * N_LEAF)).reshape((LEVELS, N_LEAF, NB)).astype(jnp.int32),
        "cross_map": jax.vmap(lambda own: jax.random.permutation(own, NB))(jax.random.split(arg_keys[2], LEVELS * N_LEAF)).reshape((LEVELS, N_LEAF, NB)).astype(jnp.int32),
        "pivot_inverse": bell_draw(arg_keys[3], (INVERSES, PANEL, PANEL), (16 * PANEL * PANEL) ** -0.5, 0.0029296875),
    }


def reference(child_front, own_map, cross_map, pivot_inverse):
    leaf_count = N_LEAF
    front_slab = child_front
    offsets = (0, 4, 6)
    for level_index in range(3):
        group_size = leaf_count // 2 ** (2 - level_index)
        share_rows = PANEL // group_size
        sibling_bit = LEAF_BITS - 3 + level_index
        blocks = front_slab.reshape(leaf_count, NB, BLOCK, NF)
        partner = jnp.take(blocks, jnp.arange(leaf_count, dtype=jnp.int32) ^ (1 << sibling_bit), axis=0)
        own_part = jnp.take_along_axis(blocks, own_map[level_index][:, :, None, None].astype(jnp.int32), axis=1)
        cross_part = jnp.take_along_axis(partner, cross_map[level_index][:, :, None, None].astype(jnp.int32), axis=1)
        parent = (own_part.astype(jnp.float32) + cross_part.astype(jnp.float32)).astype(jnp.bfloat16)
        parent = parent.reshape(leaf_count, ROWS_DEV, NF)
        fronts = leaf_count // group_size
        pivots = parent[:, :share_rows, :].reshape(fronts, PANEL, NF)
        inverse = pivot_inverse[offsets[level_index]:offsets[level_index] + fronts]

        def solve_one(operands):
            return jnp.dot(operands[0], operands[1], preferred_element_type=jnp.float32).astype(jnp.bfloat16)

        upper_rows = lax.map(solve_one, (inverse, pivots))

        def update(device):
            slab_rows = parent[device]
            upper_now = upper_rows[device // group_size]
            reduced = slab_rows.astype(jnp.float32) - jnp.dot(slab_rows[:, :PANEL], upper_now, preferred_element_type=jnp.float32)
            keep_mask = jnp.arange(ROWS_DEV, dtype=jnp.int32)[:, None] >= share_rows
            return jnp.where(keep_mask, reduced, jnp.zeros_like(reduced)).astype(jnp.bfloat16)

        front_slab = lax.map(update, jnp.arange(leaf_count, dtype=jnp.int32)).reshape(leaf_count * ROWS_DEV, NF)
    return front_slab
```

```python
import functools

import jax
import jax.numpy as jnp
from jax import lax
from jax.experimental import pallas as pl
from jax.experimental.pallas import tpu as pltpu
from jax.sharding import PartitionSpec as P

PANEL = 512
BLOCK = 128
WIDTH = 256
MESH = pl.DeviceIdType.MESH
F32 = jnp.float32
BF16 = jnp.bfloat16


def multiple(value, of):
    return pl.multiple_of(value, of)


def kernel(
    child, maps, inverse, out,
    front, parent, pfront, pparent, inv, map_buf, map_tab,
    piv0, piv1, piv2, ppiv0, ppiv1, upper, pupper0, pupper1,
    map_send, map_recv, a2a_send, a2a_recv, first_send, first_recv,
    pan_send, pan_recv, fwd_send, fwd_recv, piv0_send, piv0_recv,
    piv1_send, piv1_recv, piv2_send, piv2_recv, pp0_send, pp0_recv,
    pp1_send, pp1_recv, up0_send, up0_recv, up0f_send, up0f_recv,
    up1_send, up1_recv, up1f_send, up1f_recv, out_send, out_recv, local_sem,
):
    leaf = lax.axis_index("leaf")
    panel = lax.axis_index("panel")
    g, r = leaf // 4, leaf % 4
    y, x = g // 4, g % 4
    core = panel % 2
    mate = panel + 1 - 2 * core

    def at(dy, dx):
        return ((y + dy) % 4) * 4 + (x + dx) % 4

    def each_peer(stage, visit):
        if stage == 0:
            @pl.loop(1, 4)
            def _(i):
                visit(0, i)
        elif stage == 1:
            @pl.loop(0, 4)
            def _(i):
                visit(1, i)
                visit(3, i)
        else:
            @pl.loop(0, 4)
            def _(i):
                visit(2, i)

    def remote(src, dst, send, recv, to_leaf, to_panel):
        return pltpu.make_async_remote_copy(
            src_ref=src, dst_ref=dst, send_sem=send, recv_sem=recv,
            device_id=(to_leaf, to_panel), device_id_type=MESH,
        )

    barrier = pltpu.get_barrier_semaphore()

    def greet(dy, dx):
        pl.semaphore_signal(barrier, inc=1, device_id=(at(dy, dx) * 4 + r, panel), device_id_type=MESH)

    for stage in range(3):
        each_peer(stage, greet)

    @pl.loop(1, 4)
    def _(i):
        pl.semaphore_signal(barrier, inc=1, device_id=(g * 4 + (r + i) % 4, panel), device_id_type=MESH)
        pl.semaphore_signal(barrier, inc=1, device_id=(leaf, (panel + i) % 4), device_id_type=MESH)

    def columns(which):
        return pl.ds(multiple(which * WIDTH, WIDTH), WIDTH)

    own_copy = pltpu.make_async_copy(child.at[:, :, columns(g)], front.at[g], local_sem.at[0])
    own_copy.start()
    inv_copy = pltpu.make_async_copy(inverse, inv, local_sem.at[1])
    inv_copy.start()
    map_copy = pltpu.make_async_copy(maps, map_buf.at[g], local_sem.at[2])
    map_copy.start()
    pl.semaphore_wait(barrier, 21)

    def first_copy(half, to_panel, index):
        return remote(
            child.at[half, :, pl.ds(0, PANEL)], pfront.at[g, half],
            first_send.at[index], first_recv.at[0], leaf, to_panel,
        )

    first_own = pltpu.make_async_copy(child.at[0, :, pl.ds(0, PANEL)], pfront.at[g, 0], local_sem.at[3])

    @pl.when(panel == 0)
    def _():
        first_copy(0, 2, 1).start()
        first_copy(1, 3, 2).start()
        first_copy(1, 1, 0).start()
        first_own.start()

    def map_of(slab, to):
        return remote(maps, map_buf.at[slab], map_send.at[to], map_recv.at[slab], to * 4 + r, panel)

    def a2a_of(slab, to):
        return remote(child.at[:, :, columns(to)], front.at[slab], a2a_send.at[to], a2a_recv.at[slab], to * 4 + r, panel)

    def pan_of(slab, to):
        return remote(pfront.at[slab, core], pfront.at[slab, core], pan_send.at[to], pan_recv.at[slab], to * 4 + r, panel)

    def send_child(dy, dx):
        to = at(dy, dx)
        map_of(g, to).start()
        a2a_of(g, to).start()

    def send_panel(dy, dx):
        pan_of(g, at(dy, dx)).start()

    each_peer(0, send_child)

    @pl.when(panel == 0)
    def _():
        first_own.wait()

    @pl.when(panel != 0)
    def _():
        first_copy(core, panel, 0).wait_recv()

    each_peer(0, send_panel)
    each_peer(1, send_child)
    each_peer(1, send_panel)
    each_peer(2, send_child)
    each_peer(2, send_panel)

    own_copy.wait()
    map_copy.wait()

    def take_map(dy, dx):
        map_of(at(dy, dx), g).wait_recv()

    for stage in range(3):
        each_peer(stage, take_map)
    to_smem = pltpu.make_async_copy(map_buf, map_tab, local_sem.at[2])
    to_smem.start()
    to_smem.wait()

    def extend(src, dst, level, a, b):
        width = src.shape[3]
        for mine, other in ((a, b), (b, a)):
            for slot in range(2):
                from_own = map_tab[mine, level, slot] == 0
                from_cross = map_tab[mine, level, 2 + slot] == 0
                for low in range(0, BLOCK, 32):
                    for left in range(0, width, WIDTH):
                        part = (pl.ds(low, 32), pl.ds(left, WIDTH))
                        kept = jnp.where(from_own, src[(mine, 0) + part], src[(mine, 1) + part])
                        moved = jnp.where(from_cross, src[(other, 0) + part], src[(other, 1) + part])
                        dst[(mine, slot) + part] = (kept.astype(F32) + moved.astype(F32)).astype(BF16)

    def subtract(src, dst, factor, top, slab, rows):
        width = src.shape[3]
        left = pparent[slab].reshape(2 * BLOCK, PANEL)
        keep = lax.broadcasted_iota(jnp.int32, (2 * BLOCK, WIDTH), 0) >= rows
        for low in range(0, width, WIDTH):
            part = pl.ds(low, WIDTH)
            product = jnp.dot(left, factor[top, :, part], preferred_element_type=F32)
            start = src[slab, :, :, part].reshape(2 * BLOCK, WIDTH).astype(F32)
            reduced = jnp.where(keep, start - product, 0.0).astype(BF16)
            dst[slab, :, :, part] = reduced.reshape(2, BLOCK, WIDTH)

    def piv0_of(f, owner, to):
        slabs = pl.ds(f * 4, 4)
        return remote(
            parent.at[slabs, 0, pl.ds(0, 32), :], piv0.at[slabs, owner],
            piv0_send.at[f, to], piv0_recv.at[f, owner], g * 4 + to, panel,
        )

    def fwd_of(f, half):
        part = pfront.at[pl.ds(f * 4, 4), half]
        return remote(part, part, fwd_send.at[f], fwd_recv.at[f], leaf, mate)

    def open_front(f):
        fwd_of(f, core).start()

        @pl.loop(0, 2)
        def _(j):
            extend(front, parent, 0, f * 4 + j, f * 4 + j + 2)

        @pl.loop(1, 4)
        def _(i):
            piv0_of(f, r, (r + i) % 4).start()

        @pl.loop(0, 4)
        def _(j):
            piv0[f * 4 + j, r] = parent[f * 4 + j, 0, 0:32, :]

    def open_panel(f):
        fwd_of(f, 1 - core).wait_recv()

        @pl.loop(0, 2)
        def _(j):
            extend(pfront, pparent, 0, f * 4 + j, f * 4 + j + 2)

    def take_slab(dy, dx):
        a2a_of(at(dy, dx), g).wait_recv()
        pan_of(at(dy, dx), g).wait_recv()

    piece = pl.ds(multiple(x * BLOCK, BLOCK), BLOCK)

    def pp0_of(owner, to):
        return remote(
            pparent.at[pl.ds(y * 4, 4), 0, pl.ds(0, 32), piece], ppiv0.at[:, owner],
            pp0_send.at[to], pp0_recv.at[owner], g * 4 + to, panel,
        )

    def up0_of(slab, to):
        part = pupper0.at[
            slab // 4, pl.ds(multiple(core * 256, 256), 256), pl.ds(multiple(slab % 4 * BLOCK, BLOCK), BLOCK)
        ]
        return remote(part, part, up0_send.at[to], up0_recv.at[slab], to * 4 + r, panel)

    def up0f_of(f, half):
        part = pupper0.at[f, pl.ds(multiple(half * 256, 256), 256), :]
        return remote(part, part, up0f_send.at[f], up0f_recv.at[f], leaf, mate)

    each_peer(0, take_slab)
    open_front(y)
    open_panel(y)

    @pl.loop(1, 4)
    def _(i):
        pp0_of(r, (r + i) % 4).start()

    @pl.loop(0, 4)
    def _(j):
        ppiv0[j, r] = pparent[y * 4 + j, 0, 0:32, piece]

    inv_copy.wait()

    @pl.loop(1, 4)
    def _(i):
        pp0_of((r + i) % 4, r).wait_recv()

    half0 = pl.ds(multiple(core * 256, 256), 256)
    pupper0[y, half0, piece] = jnp.dot(
        inv[y, half0, :], ppiv0[...].reshape(PANEL, BLOCK), preferred_element_type=F32
    ).astype(BF16)
    for stage in range(3):
        each_peer(stage, lambda dy, dx: up0_of(g, at(dy, dx)).start())

    each_peer(1, take_slab)
    open_front((y + 1) % 4)
    open_front((y + 3) % 4)
    open_panel((y + 1) % 4)
    open_panel((y + 3) % 4)
    each_peer(2, take_slab)
    open_front((y + 2) % 4)
    open_panel((y + 2) % 4)

    each_peer(0, lambda dy, dx: up0_of(at(dy, dx), g).wait_recv())
    up0f_of(y, core).start()
    each_peer(1, lambda dy, dx: up0_of(at(dy, dx), g).wait_recv())
    up0f_of((y + 1) % 4, core).start()
    up0f_of((y + 3) % 4, core).start()
    each_peer(2, lambda dy, dx: up0_of(at(dy, dx), g).wait_recv())
    up0f_of((y + 2) % 4, core).start()

    @pl.when(panel == 0)
    def _():
        for index in range(3):
            first_copy(0, 1, index).wait_send()

    for stage in range(3):
        each_peer(stage, lambda dy, dx: pan_of(g, at(dy, dx)).wait_send())

    @pl.loop(0, 4)
    def _(f):
        fwd_of(f, core).wait_send()

    @pl.loop(0, 4)
    def _(f):
        up0f_of(f, 1 - core).wait_recv()

        @pl.loop(0, 4)
        def _(j):
            subtract(pparent, pfront, pupper0, f, f * 4 + j, 32)

    @pl.loop(0, 4)
    def _(f):
        @pl.loop(1, 4)
        def _(i):
            piv0_of(f, (r + i) % 4, r).wait_recv()

        upper[f] = jnp.dot(
            inv[f], piv0[pl.ds(f * 4, 4)].reshape(PANEL, WIDTH), preferred_element_type=F32
        ).astype(BF16)

        @pl.loop(0, 4)
        def _(j):
            subtract(parent, front, upper, f, f * 4 + j, 32)

    @pl.loop(0, 4)
    def _(f):
        @pl.loop(1, 4)
        def _(i):
            piv0_of(f, r, (r + i) % 4).wait_send()

    @pl.loop(1, 4)
    def _(i):
        pp0_of(r, (r + i) % 4).wait_send()

    def piv1_of(owner, to):
        return remote(
            parent.at[:, 0, pl.ds(0, 16), :], piv1.at[:, owner],
            piv1_send.at[to], piv1_recv.at[owner], g * 4 + to, panel,
        )

    def pp1_of(owner, to):
        return remote(
            pparent.at[pl.ds(y // 2 * 8, 8), 0, pl.ds(0, 16), piece], ppiv1.at[:, owner],
            pp1_send.at[to], pp1_recv.at[owner], g * 4 + to, panel,
        )

    def up1_of(slab, to):
        part = pupper1.at[
            slab // 8,
            pl.ds(multiple(core * 256 + slab // 4 % 2 * BLOCK, BLOCK), BLOCK),
            pl.ds(multiple(slab % 4 * BLOCK, BLOCK), BLOCK),
        ]
        return remote(part, part, up1_send.at[to], up1_recv.at[slab], to * 4 + r, panel)

    def up1f_of(f, half):
        part = pupper1.at[f, pl.ds(multiple(half * 256, 256), 256), :]
        return remote(part, part, up1f_send.at[f], up1f_recv.at[f], leaf, mate)

    @pl.loop(0, 2)
    def _(f):
        @pl.loop(0, 4)
        def _(j):
            extend(front, parent, 1, f * 8 + j, f * 8 + j + 4)

    @pl.loop(1, 4)
    def _(i):
        piv1_of(r, (r + i) % 4).start()

    @pl.loop(0, 16)
    def _(j):
        piv1[j, r] = parent[j, 0, 0:16, :]

    @pl.loop(0, 2)
    def _(f):
        @pl.loop(0, 4)
        def _(j):
            extend(pfront, pparent, 1, f * 8 + j, f * 8 + j + 4)

    @pl.loop(1, 4)
    def _(i):
        pp1_of(r, (r + i) % 4).start()

    @pl.loop(0, 8)
    def _(j):
        ppiv1[j, r] = pparent[y // 2 * 8 + j, 0, 0:16, piece]

    @pl.loop(1, 4)
    def _(i):
        pp1_of((r + i) % 4, r).wait_recv()

    quarter = pl.ds(multiple(core * 256 + y % 2 * BLOCK, BLOCK), BLOCK)
    pupper1[y // 2, quarter, piece] = jnp.dot(
        inv[4 + y // 2, quarter, :], ppiv1[...].reshape(PANEL, BLOCK), preferred_element_type=F32
    ).astype(BF16)
    for stage in range(3):
        each_peer(stage, lambda dy, dx: up1_of(g, at(dy, dx)).start())

    @pl.loop(1, 4)
    def _(i):
        piv1_of((r + i) % 4, r).wait_recv()

    @pl.loop(0, 2)
    def _(f):
        upper[f] = jnp.dot(
            inv[4 + f], piv1[pl.ds(f * 8, 8)].reshape(PANEL, WIDTH), preferred_element_type=F32
        ).astype(BF16)

        @pl.loop(0, 8)
        def _(j):
            subtract(parent, front, upper, f, f * 8 + j, 16)

    @pl.loop(1, 4)
    def _(i):
        piv1_of(r, (r + i) % 4).wait_send()
        pp1_of(r, (r + i) % 4).wait_send()

    def piv2_of(owner, to):
        return remote(
            piv2.at[:, owner], piv2.at[:, owner],
            piv2_send.at[to], piv2_recv.at[owner], g * 4 + to, panel,
        )

    @pl.loop(0, 8)
    def _(j):
        extend(front, parent, 2, j, j + 8)

    @pl.loop(0, 16)
    def _(j):
        piv2[j, r] = parent[j, 0, 0:16, :].astype(F32)[0:8]

    @pl.loop(1, 4)
    def _(i):
        piv2_of(r, (r + i) % 4).start()

    for stage in range(3):
        each_peer(stage, lambda dy, dx: up1_of(at(dy, dx), g).wait_recv())

    @pl.loop(0, 2)
    def _(f):
        up1f_of(f, core).start()

    @pl.loop(0, 2)
    def _(f):
        up1f_of(f, 1 - core).wait_recv()

        @pl.loop(0, 8)
        def _(j):
            subtract(pparent, pfront, pupper1, f, f * 8 + j, 16)

    @pl.loop(0, 8)
    def _(j):
        extend(pfront, pparent, 2, j, j + 8)

    @pl.loop(1, 4)
    def _(i):
        piv2_of((r + i) % 4, r).wait_recv()

    upper[0] = jnp.dot(
        inv[6], piv2[...].reshape(PANEL, WIDTH).astype(BF16), preferred_element_type=F32
    ).astype(BF16)

    def out_of(slab, to):
        return remote(
            front.at[to], out.at[:, :, columns(slab)],
            out_send.at[to], out_recv.at[slab], to * 4 + r, panel,
        )

    def finish(dy, dx):
        to = at(dy, dx)
        subtract(parent, front, upper, 0, to, 8)
        out_of(g, to).start()

    for stage in (2, 1, 0):
        each_peer(stage, finish)
    subtract(parent, front, upper, 0, g, 8)
    out_copy = pltpu.make_async_copy(front.at[g], out.at[:, :, columns(g)], local_sem.at[0])
    out_copy.start()
    out_copy.wait()

    def settle(dy, dx):
        slab = at(dy, dx)
        out_of(slab, g).wait_recv()
        out_of(g, slab).wait_send()
        a2a_of(g, slab).wait_send()
        map_of(g, slab).wait_send()
        up0_of(g, slab).wait_send()
        up1_of(g, slab).wait_send()

    for stage in range(3):
        each_peer(stage, settle)

    @pl.loop(0, 4)
    def _(f):
        up0f_of(f, core).wait_send()

    @pl.loop(0, 2)
    def _(f):
        up1f_of(f, core).wait_send()

    @pl.loop(1, 4)
    def _(i):
        piv2_of(r, (r + i) % 4).wait_send()


def on_device(child_front, own_map, cross_map, pivot_inverse):
    rows, width = child_front.shape
    maps = jnp.concatenate([own_map[:, 0, :], cross_map[:, 0, :]], axis=1)
    maps = jnp.pad(maps, ((0, 8 - maps.shape[0]), (0, 128 - maps.shape[1])))
    dma = pltpu.SemaphoreType.DMA
    call = pl.pallas_call(
        kernel,
        out_shape=jax.ShapeDtypeStruct((2, BLOCK, width), BF16),
        in_specs=[
            pl.BlockSpec(memory_space=pl.ANY),
            pl.BlockSpec(memory_space=pltpu.VMEM),
            pl.BlockSpec(memory_space=pl.ANY),
        ],
        out_specs=pl.BlockSpec(memory_space=pl.ANY),
        scratch_shapes=[
            pltpu.VMEM((16, 2, BLOCK, WIDTH), BF16),
            pltpu.VMEM((16, 2, BLOCK, WIDTH), BF16),
            pltpu.VMEM((16, 2, BLOCK, PANEL), BF16),
            pltpu.VMEM((16, 2, BLOCK, PANEL), BF16),
            pltpu.VMEM((7, PANEL, PANEL), BF16),
            pltpu.VMEM((16, 8, 128), jnp.int32),
            pltpu.SMEM((16, 8, 128), jnp.int32),
            pltpu.VMEM((16, 4, 32, WIDTH), BF16),
            pltpu.VMEM((16, 4, 16, WIDTH), BF16),
            pltpu.VMEM((16, 4, 8, WIDTH), F32),
            pltpu.VMEM((4, 4, 32, BLOCK), BF16),
            pltpu.VMEM((8, 4, 16, BLOCK), BF16),
            pltpu.VMEM((4, PANEL, WIDTH), BF16),
            pltpu.VMEM((4, PANEL, PANEL), BF16),
            pltpu.VMEM((2, PANEL, PANEL), BF16),
            dma((16,)), dma((16,)), dma((16,)), dma((16,)), dma((3,)), dma((1,)),
            dma((16,)), dma((16,)), dma((4,)), dma((4,)), dma((4, 4)), dma((4, 4)),
            dma((4,)), dma((4,)), dma((4,)), dma((4,)), dma((4,)), dma((4,)),
            dma((4,)), dma((4,)), dma((16,)), dma((16,)), dma((4,)), dma((4,)),
            dma((16,)), dma((16,)), dma((2,)), dma((2,)), dma((16,)), dma((16,)), dma((4,)),
        ],
        compiler_params=pltpu.CompilerParams(
            collective_id=0, has_side_effects=True, vmem_limit_bytes=48 * 1024 * 1024
        ),
        cost_estimate=pl.CostEstimate(
            flops=9_000_000_000, bytes_accessed=16_000_000, transcendentals=0
        ),
    )
    result = call(child_front.reshape(2, BLOCK, width), maps, pivot_inverse)
    return result.reshape(rows, width)


def solution(mesh):
    placed = (P("leaf", "panel"), P(None, "leaf", None), P(None, "leaf", None), P())
    return jax.shard_map(
        on_device, mesh=mesh, in_specs=placed, out_specs=P("leaf", "panel"), check_vma=False
    )
```

```python
import functools

import jax
import jax.numpy as jnp
from jax import lax
from jax.experimental import pallas as pl
from jax.experimental.pallas import tpu as pltpu
from jax.sharding import PartitionSpec as P

PANEL = 512
BLOCK = 128
WIDTH = 256
MESH = pl.DeviceIdType.MESH
F32 = jnp.float32
BF16 = jnp.bfloat16


def multiple(value, of):
    return pl.multiple_of(value, of)


def kernel(
    child, maps, inverse, out,
    front, parent, pfront, pparent, inv, map_buf, map_tab,
    piv0, piv1, piv2, piv2_wide, ppiv0, ppiv1, upper, pupper0, pupper1,
    map_send, map_recv, a2a_send, a2a_recv, first_send, first_recv,
    pan_send, pan_recv, fwd_send, fwd_recv, piv0_send, piv0_recv,
    piv1_send, piv1_recv, piv2_send, piv2_recv, pp0_send, pp0_recv,
    pp1_send, pp1_recv, up0_send, up0_recv, up0f_send, up0f_recv,
    up1_send, up1_recv, up1f_send, up1f_recv, out_send, out_recv, local_sem,
):
    leaf = lax.axis_index("leaf")
    panel = lax.axis_index("panel")
    g, r = leaf // 4, leaf % 4
    y, x = g // 4, g % 4
    core = panel % 2
    mate = panel + 1 - 2 * core

    def at(dy, dx):
        return ((y + dy) % 4) * 4 + (x + dx) % 4

    def each_peer(stage, visit):
        if stage == 0:
            @pl.loop(1, 4)
            def _(i):
                visit(0, i)
        elif stage == 1:
            @pl.loop(0, 4)
            def _(i):
                visit(1, i)
                visit(3, i)
        else:
            @pl.loop(0, 4)
            def _(i):
                visit(2, i)

    def remote(src, dst, send, recv, to_leaf, to_panel):
        return pltpu.make_async_remote_copy(
            src_ref=src, dst_ref=dst, send_sem=send, recv_sem=recv,
            device_id=(to_leaf, to_panel), device_id_type=MESH,
        )

    def crossed(first, second):
        return at(core * first + (1 - core) * second, core * second + (1 - core) * first)

    class Spread:
        def __init__(self, part_of, send, recv):
            self.part_of, self.send, self.recv = part_of, send, recv

        def copy(self, slab, i, j, to):
            part = self.part_of(slab)
            return remote(part, part, self.send.at[i, j], self.recv.at[slab], to * 4 + r, panel)

        def begin(self):
            @pl.loop(1, 4)
            def _(i):
                self.copy(g, i, 0, crossed(i, 0)).start()
                self.copy(g, 0, i, crossed(0, i)).start()

        def pass_on(self):
            @pl.loop(1, 4)
            def _(i):
                slab = crossed(i, 0)
                self.copy(slab, 0, 0, g).wait_recv()

                @pl.loop(1, 4)
                def _(j):
                    self.copy(slab, i, j, crossed(0, j)).start()

        def take_direct(self):
            @pl.loop(1, 4)
            def _(j):
                self.copy(crossed(0, j), 0, 0, g).wait_recv()

        def take_passed(self):
            @pl.loop(1, 4)
            def _(i):
                @pl.loop(1, 4)
                def _(j):
                    self.copy(crossed(i, j), 0, 0, g).wait_recv()

        def sent(self):
            @pl.loop(1, 4)
            def _(i):
                self.copy(g, i, 0, crossed(i, 0)).wait_send()
                self.copy(g, 0, i, crossed(0, i)).wait_send()

                @pl.loop(1, 4)
                def _(j):
                    self.copy(crossed(i, 0), i, j, crossed(0, j)).wait_send()

    barrier = pltpu.get_barrier_semaphore()

    def greet(dy, dx):
        pl.semaphore_signal(barrier, inc=1, device_id=(at(dy, dx) * 4 + r, panel), device_id_type=MESH)

    for stage in range(3):
        each_peer(stage, greet)

    @pl.loop(1, 4)
    def _(i):
        pl.semaphore_signal(barrier, inc=1, device_id=(g * 4 + (r + i) % 4, panel), device_id_type=MESH)
        pl.semaphore_signal(barrier, inc=1, device_id=(leaf, (panel + i) % 4), device_id_type=MESH)

    def columns(which):
        return pl.ds(multiple(which * WIDTH, WIDTH), WIDTH)

    own_copy = pltpu.make_async_copy(child.at[:, :, columns(g)], front.at[g], local_sem.at[0])
    own_copy.start()
    inv_copy = pltpu.make_async_copy(inverse, inv, local_sem.at[1])
    inv_copy.start()
    map_copy = pltpu.make_async_copy(maps, map_buf.at[g], local_sem.at[2])
    map_copy.start()
    pl.semaphore_wait(barrier, 21)

    def first_copy(half, to_panel, index):
        return remote(
            child.at[half, :, pl.ds(0, PANEL)], pfront.at[g, half],
            first_send.at[index], first_recv.at[0], leaf, to_panel,
        )

    first_own = pltpu.make_async_copy(child.at[0, :, pl.ds(0, PANEL)], pfront.at[g, 0], local_sem.at[3])

    @pl.when(panel == 0)
    def _():
        first_copy(0, 2, 1).start()
        first_copy(1, 3, 2).start()
        first_copy(1, 1, 0).start()
        first_own.start()

    def map_of(slab, to):
        return remote(maps, map_buf.at[slab], map_send.at[to], map_recv.at[slab], to * 4 + r, panel)

    def a2a_of(slab, to):
        return remote(child.at[:, :, columns(to)], front.at[slab], a2a_send.at[to], a2a_recv.at[slab], to * 4 + r, panel)

    spread_panel = Spread(lambda slab: pfront.at[slab, core], pan_send, pan_recv)

    def send_child(dy, dx):
        to = at(dy, dx)
        map_of(g, to).start()
        a2a_of(g, to).start()

    each_peer(0, send_child)

    @pl.when(panel == 0)
    def _():
        first_own.wait()

    @pl.when(panel != 0)
    def _():
        first_copy(core, panel, 0).wait_recv()

    spread_panel.begin()
    each_peer(1, send_child)
    each_peer(2, send_child)

    own_copy.wait()
    map_copy.wait()

    def take_map(dy, dx):
        map_of(at(dy, dx), g).wait_recv()

    for stage in range(3):
        each_peer(stage, take_map)
    to_smem = pltpu.make_async_copy(map_buf, map_tab, local_sem.at[2])
    to_smem.start()
    to_smem.wait()

    def extend(src, dst, level, a, b):
        width = src.shape[3]
        for mine, other in ((a, b), (b, a)):
            for slot in range(2):
                from_own = map_tab[mine, level, slot] == 0
                from_cross = map_tab[mine, level, 2 + slot] == 0
                for low in range(0, BLOCK, 32):
                    for left in range(0, width, WIDTH):
                        part = (pl.ds(low, 32), pl.ds(left, WIDTH))
                        kept = jnp.where(from_own, src[(mine, 0) + part], src[(mine, 1) + part])
                        moved = jnp.where(from_cross, src[(other, 0) + part], src[(other, 1) + part])
                        dst[(mine, slot) + part] = (kept.astype(F32) + moved.astype(F32)).astype(BF16)

    def subtract(src, dst, factor, top, slab, rows):
        width = src.shape[3]
        left = pparent[slab].reshape(2 * BLOCK, PANEL)
        keep = lax.broadcasted_iota(jnp.int32, (2 * BLOCK, WIDTH), 0) >= rows
        for low in range(0, width, WIDTH):
            part = pl.ds(low, WIDTH)
            product = jnp.dot(left, factor[top, :, part], preferred_element_type=F32)
            start = src[slab, :, :, part].reshape(2 * BLOCK, WIDTH).astype(F32)
            reduced = jnp.where(keep, start - product, 0.0).astype(BF16)
            dst[slab, :, :, part] = reduced.reshape(2, BLOCK, WIDTH)

    def piv0_of(f, owner, to):
        slabs = pl.ds(f * 4, 4)
        return remote(
            parent.at[slabs, 0, pl.ds(0, 32), :], piv0.at[slabs, owner],
            piv0_send.at[f, to], piv0_recv.at[f, owner], g * 4 + to, panel,
        )

    def fwd_of(f, half):
        part = pfront.at[pl.ds(f * 4, 4), half]
        return remote(part, part, fwd_send.at[f], fwd_recv.at[f], leaf, mate)

    def open_front(f):
        @pl.loop(0, 2)
        def _(j):
            extend(front, parent, 0, f * 4 + j, f * 4 + j + 2)

        @pl.loop(1, 4)
        def _(i):
            piv0_of(f, r, (r + i) % 4).start()

        @pl.loop(0, 4)
        def _(j):
            piv0[f * 4 + j, r] = parent[f * 4 + j, 0, 0:32, :]

    def open_panel(f):
        fwd_of(f, 1 - core).wait_recv()

        @pl.loop(0, 2)
        def _(j):
            extend(pfront, pparent, 0, f * 4 + j, f * 4 + j + 2)

    def take_slab(dy, dx):
        a2a_of(at(dy, dx), g).wait_recv()

    piece = pl.ds(multiple(x * BLOCK, BLOCK), BLOCK)

    def pp0_of(owner, to):
        return remote(
            pparent.at[pl.ds(y * 4, 4), 0, pl.ds(0, 32), piece], ppiv0.at[:, owner],
            pp0_send.at[to], pp0_recv.at[owner], g * 4 + to, panel,
        )

    spread_upper0 = Spread(
        lambda slab: pupper0.at[
            slab // 4, pl.ds(multiple(core * 256, 256), 256), pl.ds(multiple(slab % 4 * BLOCK, BLOCK), BLOCK)
        ],
        up0_send, up0_recv,
    )

    def up0f_of(f, half):
        part = pupper0.at[f, pl.ds(multiple(half * 256, 256), 256), :]
        return remote(part, part, up0f_send.at[f], up0f_recv.at[f], leaf, mate)

    each_peer(0, take_slab)
    open_front(y)
    spread_panel.pass_on()
    spread_panel.take_direct()
    fwd_of(y, core).start()
    open_panel(y)

    @pl.loop(1, 4)
    def _(i):
        pp0_of(r, (r + i) % 4).start()

    @pl.loop(0, 4)
    def _(j):
        ppiv0[j, r] = pparent[y * 4 + j, 0, 0:32, piece]

    each_peer(1, take_slab)
    open_front((y + 1) % 4)
    open_front((y + 3) % 4)
    inv_copy.wait()

    @pl.loop(1, 4)
    def _(i):
        pp0_of((r + i) % 4, r).wait_recv()

    half0 = pl.ds(multiple(core * 256, 256), 256)
    pupper0[y, half0, piece] = jnp.dot(
        inv[y, half0, :], ppiv0[...].reshape(PANEL, BLOCK), preferred_element_type=F32
    ).astype(BF16)
    spread_upper0.begin()

    each_peer(2, take_slab)
    open_front((y + 2) % 4)
    spread_panel.take_passed()

    @pl.loop(1, 4)
    def _(i):
        fwd_of((y + i) % 4, core).start()

    @pl.loop(1, 4)
    def _(i):
        open_panel((y + i) % 4)

    spread_upper0.pass_on()

    @pl.loop(0, 4)
    def _(i):
        f = (y + i + i // 2 - 2 * (i // 3)) % 4

        @pl.loop(1, 4)
        def _(i):
            piv0_of(f, (r + i) % 4, r).wait_recv()

        upper[f] = jnp.dot(
            inv[f], piv0[pl.ds(f * 4, 4)].reshape(PANEL, WIDTH), preferred_element_type=F32
        ).astype(BF16)

        @pl.loop(0, 4)
        def _(j):
            subtract(parent, front, upper, f, f * 4 + j, 32)

    @pl.loop(0, 4)
    def _(f):
        @pl.loop(1, 4)
        def _(i):
            piv0_of(f, r, (r + i) % 4).wait_send()

    def piv1_of(owner, to):
        return remote(
            parent.at[:, 0, pl.ds(0, 16), :], piv1.at[:, owner],
            piv1_send.at[to], piv1_recv.at[owner], g * 4 + to, panel,
        )

    def pp1_of(owner, to):
        return remote(
            pparent.at[pl.ds(y // 2 * 8, 8), 0, pl.ds(0, 16), piece], ppiv1.at[:, owner],
            pp1_send.at[to], pp1_recv.at[owner], g * 4 + to, panel,
        )

    spread_upper1 = Spread(
        lambda slab: pupper1.at[
            slab // 8,
            pl.ds(multiple(core * 256 + slab // 4 % 2 * BLOCK, BLOCK), BLOCK),
            pl.ds(multiple(slab % 4 * BLOCK, BLOCK), BLOCK),
        ],
        up1_send, up1_recv,
    )

    def up1f_of(f, half):
        part = pupper1.at[f, pl.ds(multiple(half * 256, 256), 256), :]
        return remote(part, part, up1f_send.at[f], up1f_recv.at[f], leaf, mate)

    @pl.loop(0, 2)
    def _(f):
        @pl.loop(0, 4)
        def _(j):
            extend(front, parent, 1, f * 8 + j, f * 8 + j + 4)

    @pl.loop(1, 4)
    def _(i):
        piv1_of(r, (r + i) % 4).start()

    @pl.loop(0, 16)
    def _(j):
        piv1[j, r] = parent[j, 0, 0:16, :]

    spread_upper0.take_direct()
    spread_upper0.take_passed()

    @pl.loop(0, 4)
    def _(f):
        up0f_of(f, core).start()

    @pl.when(panel == 0)
    def _():
        for index in range(3):
            first_copy(0, 1, index).wait_send()

    spread_panel.sent()

    @pl.loop(0, 4)
    def _(f):
        fwd_of(f, core).wait_send()

    @pl.loop(1, 4)
    def _(i):
        pp0_of(r, (r + i) % 4).wait_send()

    @pl.loop(0, 4)
    def _(f):
        up0f_of(f, 1 - core).wait_recv()

        @pl.loop(0, 4)
        def _(j):
            subtract(pparent, pfront, pupper0, f, f * 4 + j, 32)

    @pl.loop(0, 2)
    def _(f):
        @pl.loop(0, 4)
        def _(j):
            extend(pfront, pparent, 1, f * 8 + j, f * 8 + j + 4)

    @pl.loop(1, 4)
    def _(i):
        pp1_of(r, (r + i) % 4).start()

    @pl.loop(0, 8)
    def _(j):
        ppiv1[j, r] = pparent[y // 2 * 8 + j, 0, 0:16, piece]

    @pl.loop(1, 4)
    def _(i):
        piv1_of((r + i) % 4, r).wait_recv()

    @pl.loop(0, 2)
    def _(f):
        upper[f] = jnp.dot(
            inv[4 + f], piv1[pl.ds(f * 8, 8)].reshape(PANEL, WIDTH), preferred_element_type=F32
        ).astype(BF16)

    @pl.loop(1, 4)
    def _(i):
        pp1_of((r + i) % 4, r).wait_recv()

    quarter = pl.ds(multiple(core * 256 + y % 2 * BLOCK, BLOCK), BLOCK)
    pupper1[y // 2, quarter, piece] = jnp.dot(
        inv[4 + y // 2, quarter, :], ppiv1[...].reshape(PANEL, BLOCK), preferred_element_type=F32
    ).astype(BF16)
    spread_upper1.begin()

    @pl.loop(0, 2)
    def _(f):
        @pl.loop(0, 8)
        def _(j):
            subtract(parent, front, upper, f, f * 8 + j, 16)

    @pl.loop(1, 4)
    def _(i):
        piv1_of(r, (r + i) % 4).wait_send()
        pp1_of(r, (r + i) % 4).wait_send()

    def piv2_of(owner, to):
        return remote(
            piv2.at[owner], piv2.at[owner], piv2_send.at[to], piv2_recv.at[owner], g * 4 + to, panel,
        )

    @pl.loop(0, 8)
    def _(j):
        extend(front, parent, 2, j, j + 8)

    @pl.loop(0, 8)
    def _(j):
        pair = [parent[2 * j + k, 0, 0:16, :].astype(F32)[0:8] for k in range(2)]
        piv2[r, j] = jnp.concatenate(pair, axis=0).astype(BF16)

    @pl.loop(1, 4)
    def _(i):
        piv2_of(r, (r + i) % 4).start()

    spread_upper1.pass_on()
    spread_upper1.take_direct()
    spread_upper1.take_passed()

    @pl.loop(0, 2)
    def _(f):
        up1f_of(f, core).start()

    @pl.loop(0, 2)
    def _(f):
        up1f_of(f, 1 - core).wait_recv()

        @pl.loop(0, 8)
        def _(j):
            subtract(pparent, pfront, pupper1, f, f * 8 + j, 16)

    @pl.loop(0, 8)
    def _(j):
        extend(pfront, pparent, 2, j, j + 8)

    @pl.loop(1, 4)
    def _(i):
        piv2_of((r + i) % 4, r).wait_recv()

    @pl.loop(0, 4)
    def _(owner):
        @pl.loop(0, 8)
        def _(j):
            both = piv2[owner, j].astype(F32)
            piv2_wide[2 * j, owner] = both[0:8]
            piv2_wide[2 * j + 1, owner] = both[8:16]

    upper[0] = jnp.dot(
        inv[6], piv2_wide[...].reshape(PANEL, WIDTH).astype(BF16), preferred_element_type=F32
    ).astype(BF16)

    def out_of(slab, to):
        return remote(
            front.at[to], out.at[:, :, columns(slab)],
            out_send.at[to], out_recv.at[slab], to * 4 + r, panel,
        )

    def finish(dy, dx):
        to = at(dy, dx)
        subtract(parent, front, upper, 0, to, 8)
        out_of(g, to).start()

    for stage in (2, 1, 0):
        each_peer(stage, finish)
    subtract(parent, front, upper, 0, g, 8)
    out_copy = pltpu.make_async_copy(front.at[g], out.at[:, :, columns(g)], local_sem.at[0])
    out_copy.start()
    out_copy.wait()

    def settle(dy, dx):
        slab = at(dy, dx)
        out_of(slab, g).wait_recv()
        out_of(g, slab).wait_send()
        a2a_of(g, slab).wait_send()
        map_of(g, slab).wait_send()

    for stage in range(3):
        each_peer(stage, settle)

    spread_upper0.sent()
    spread_upper1.sent()

    @pl.loop(0, 4)
    def _(f):
        up0f_of(f, core).wait_send()

    @pl.loop(0, 2)
    def _(f):
        up1f_of(f, core).wait_send()

    @pl.loop(1, 4)
    def _(i):
        piv2_of(r, (r + i) % 4).wait_send()


def on_device(child_front, own_map, cross_map, pivot_inverse):
    rows, width = child_front.shape
    maps = jnp.concatenate([own_map[:, 0, :], cross_map[:, 0, :]], axis=1)
    maps = jnp.pad(maps, ((0, 8 - maps.shape[0]), (0, 128 - maps.shape[1])))
    dma = pltpu.SemaphoreType.DMA
    call = pl.pallas_call(
        kernel,
        out_shape=jax.ShapeDtypeStruct((2, BLOCK, width), BF16),
        in_specs=[
            pl.BlockSpec(memory_space=pl.ANY),
            pl.BlockSpec(memory_space=pltpu.VMEM),
            pl.BlockSpec(memory_space=pl.ANY),
        ],
        out_specs=pl.BlockSpec(memory_space=pl.ANY),
        scratch_shapes=[
            pltpu.VMEM((16, 2, BLOCK, WIDTH), BF16),
            pltpu.VMEM((16, 2, BLOCK, WIDTH), BF16),
            pltpu.VMEM((16, 2, BLOCK, PANEL), BF16),
            pltpu.VMEM((16, 2, BLOCK, PANEL), BF16),
            pltpu.VMEM((7, PANEL, PANEL), BF16),
            pltpu.VMEM((16, 8, 128), jnp.int32),
            pltpu.SMEM((16, 8, 128), jnp.int32),
            pltpu.VMEM((16, 4, 32, WIDTH), BF16),
            pltpu.VMEM((16, 4, 16, WIDTH), BF16),
            pltpu.VMEM((4, 8, 16, WIDTH), BF16),
            pltpu.VMEM((16, 4, 8, WIDTH), F32),
            pltpu.VMEM((4, 4, 32, BLOCK), BF16),
            pltpu.VMEM((8, 4, 16, BLOCK), BF16),
            pltpu.VMEM((4, PANEL, WIDTH), BF16),
            pltpu.VMEM((4, PANEL, PANEL), BF16),
            pltpu.VMEM((2, PANEL, PANEL), BF16),
            dma((16,)), dma((16,)), dma((16,)), dma((16,)), dma((3,)), dma((1,)),
            dma((4, 4)), dma((16,)), dma((4,)), dma((4,)), dma((4, 4)), dma((4, 4)),
            dma((4,)), dma((4,)), dma((4,)), dma((4,)), dma((4,)), dma((4,)),
            dma((4,)), dma((4,)), dma((4, 4)), dma((16,)), dma((4,)), dma((4,)),
            dma((4, 4)), dma((16,)), dma((2,)), dma((2,)), dma((16,)), dma((16,)), dma((4,)),
        ],
        compiler_params=pltpu.CompilerParams(
            collective_id=0, has_side_effects=True, vmem_limit_bytes=60 * 1024 * 1024
        ),
        cost_estimate=pl.CostEstimate(
            flops=9_000_000_000, bytes_accessed=16_000_000, transcendentals=0
        ),
    )
    result = call(child_front.reshape(2, BLOCK, width), maps, pivot_inverse)
    return result.reshape(rows, width)


def solution(mesh):
    placed = (P("leaf", "panel"), P(None, "leaf", None), P(None, "leaf", None), P())
    return jax.shard_map(
        on_device, mesh=mesh, in_specs=placed, out_specs=P("leaf", "panel"), check_vma=False
    )
```

```python
import functools

import jax
import jax.numpy as jnp
from jax import lax
from jax.experimental import pallas as pl
from jax.experimental.pallas import tpu as pltpu
from jax.sharding import PartitionSpec as P

PANEL = 512
BLOCK = 128
WIDTH = 256
HALF = 128
MESH = pl.DeviceIdType.MESH
F32 = jnp.float32
BF16 = jnp.bfloat16


def multiple(value, of):
    return pl.multiple_of(value, of)


def kernel(
    child, maps, inverse, out,
    front, parent, pfront, pparent0, pparent1, pparent2, inv, map_buf, map_tab,
    piv0, piv1, piv2, piv2_wide, ppiv0, ppiv1, upper, pupper0, pupper1,
    map_send, map_recv, a2a_send, a2a_recv, first_send, first_recv,
    pan_send, pan_recv, fwd_send, fwd_recv, piv0_send, piv0_recv,
    piv1_send, piv1_recv, piv2_send, piv2_recv, pp0_send, pp0_recv,
    pp1_send, pp1_recv, up0_send, up0_recv, up0f_send, up0f_recv,
    up1_send, up1_recv, up1f_send, up1f_recv, out_send, out_recv, local_sem,
):
    leaf = lax.axis_index("leaf")
    panel = lax.axis_index("panel")
    g, r = leaf // 4, leaf % 4
    y, x = g // 4, g % 4
    core = panel % 2
    mate = panel + 1 - 2 * core

    def at(dy, dx):
        return ((y + dy) % 4) * 4 + (x + dx) % 4

    def each_peer(stage, visit):
        if stage == 0:
            @pl.loop(1, 4)
            def _(i):
                visit(0, i)
        elif stage == 1:
            @pl.loop(0, 4)
            def _(i):
                visit(1, i)
                visit(3, i)
        else:
            @pl.loop(0, 4)
            def _(i):
                visit(2, i)

    def remote(src, dst, send, recv, to_leaf, to_panel):
        return pltpu.make_async_remote_copy(
            src_ref=src, dst_ref=dst, send_sem=send, recv_sem=recv,
            device_id=(to_leaf, to_panel), device_id_type=MESH,
        )

    def crossed(first, second):
        return at(core * first + (1 - core) * second, core * second + (1 - core) * first)

    class Spread:
        def __init__(self, part_of, send, recv):
            self.part_of, self.send, self.recv = part_of, send, recv

        def copy(self, slab, i, j, to):
            part = self.part_of(slab)
            return remote(part, part, self.send.at[i, j], self.recv.at[slab], to * 4 + r, panel)

        def begin(self):
            @pl.loop(1, 4)
            def _(i):
                self.copy(g, i, 0, crossed(i, 0)).start()
                self.copy(g, 0, i, crossed(0, i)).start()

        def pass_on(self):
            @pl.loop(1, 4)
            def _(i):
                slab = crossed(i, 0)
                self.copy(slab, 0, 0, g).wait_recv()

                @pl.loop(1, 4)
                def _(j):
                    self.copy(slab, i, j, crossed(0, j)).start()

        def take_direct(self):
            @pl.loop(1, 4)
            def _(j):
                self.copy(crossed(0, j), 0, 0, g).wait_recv()

        def take_passed(self):
            @pl.loop(1, 4)
            def _(i):
                @pl.loop(1, 4)
                def _(j):
                    self.copy(crossed(i, j), 0, 0, g).wait_recv()

        def sent(self):
            @pl.loop(1, 4)
            def _(i):
                self.copy(g, i, 0, crossed(i, 0)).wait_send()
                self.copy(g, 0, i, crossed(0, i)).wait_send()

                @pl.loop(1, 4)
                def _(j):
                    self.copy(crossed(i, 0), i, j, crossed(0, j)).wait_send()

    barrier = pltpu.get_barrier_semaphore()

    def greet(dy, dx):
        pl.semaphore_signal(barrier, inc=1, device_id=(at(dy, dx) * 4 + r, panel), device_id_type=MESH)

    for stage in range(3):
        each_peer(stage, greet)

    @pl.loop(1, 4)
    def _(i):
        pl.semaphore_signal(barrier, inc=1, device_id=(g * 4 + (r + i) % 4, panel), device_id_type=MESH)
        pl.semaphore_signal(barrier, inc=1, device_id=(leaf, (panel + i) % 4), device_id_type=MESH)

    def columns(which, h):
        return pl.ds(multiple(which * WIDTH + h * HALF, HALF), HALF)

    def own_copy(h):
        return pltpu.make_async_copy(child.at[:, :, columns(g, h)], front.at[h, g], local_sem.at[4 + h])

    own_copy(0).start()
    own_copy(1).start()
    inv_copy = pltpu.make_async_copy(inverse, inv, local_sem.at[1])
    inv_copy.start()
    map_copy = pltpu.make_async_copy(maps, map_buf.at[g], local_sem.at[2])
    map_copy.start()
    pl.semaphore_wait(barrier, 21)

    def first_copy(half, to_panel, index):
        return remote(
            child.at[half, :, pl.ds(0, PANEL)], pfront.at[g, half],
            first_send.at[index], first_recv.at[0], leaf, to_panel,
        )

    first_own = pltpu.make_async_copy(child.at[0, :, pl.ds(0, PANEL)], pfront.at[g, 0], local_sem.at[3])

    @pl.when(panel == 0)
    def _():
        first_copy(0, 2, 1).start()
        first_copy(1, 3, 2).start()
        first_copy(1, 1, 0).start()
        first_own.start()

    def map_of(slab, to):
        return remote(maps, map_buf.at[slab], map_send.at[to], map_recv.at[slab], to * 4 + r, panel)

    def a2a_of(h, slab, to):
        return remote(
            child.at[:, :, columns(to, h)], front.at[h, slab],
            a2a_send.at[h, to], a2a_recv.at[h, slab], to * 4 + r, panel,
        )

    spread_panel = Spread(lambda slab: pfront.at[slab, core], pan_send, pan_recv)

    def send_child(h, stage):
        each_peer(stage, lambda dy, dx: a2a_of(h, g, at(dy, dx)).start())

    for stage in range(3):
        each_peer(stage, lambda dy, dx: map_of(g, at(dy, dx)).start())
    for stage in range(3):
        send_child(0, stage)

    @pl.when(panel == 0)
    def _():
        first_own.wait()

    @pl.when(panel != 0)
    def _():
        first_copy(core, panel, 0).wait_recv()

    spread_panel.begin()

    map_copy.wait()

    def take_map(dy, dx):
        map_of(at(dy, dx), g).wait_recv()

    for stage in range(3):
        each_peer(stage, take_map)
    to_smem = pltpu.make_async_copy(map_buf, map_tab, local_sem.at[2])
    to_smem.start()
    to_smem.wait()

    def extend(src, dst, level, a, b):
        width = src.shape[3]
        step = min(width, WIDTH)
        for mine, other in ((a, b), (b, a)):
            for slot in range(2):
                from_own = map_tab[mine, level, slot] == 0
                from_cross = map_tab[mine, level, 2 + slot] == 0

                @pl.loop(0, BLOCK // 32)
                def _(q):
                    for left in range(0, width, step):
                        part = (pl.ds(multiple(q * 32, 32), 32), pl.ds(left, step))
                        kept = jnp.where(from_own, src[(mine, 0) + part], src[(mine, 1) + part])
                        moved = jnp.where(from_cross, src[(other, 0) + part], src[(other, 1) + part])
                        dst[(mine, slot) + part] = (kept.astype(F32) + moved.astype(F32)).astype(BF16)

    def subtract(src, columns_of, dst, factor, slab, rows):
        width = src.shape[3]
        step = min(width, WIDTH)
        left = columns_of[slab].reshape(2 * BLOCK, PANEL)
        keep = lax.broadcasted_iota(jnp.int32, (2 * BLOCK, step), 0) >= rows
        for low in range(0, width, step):
            part = pl.ds(low, step)
            product = jnp.dot(left, factor[:, part], preferred_element_type=F32)
            start = src[slab, :, :, part].reshape(2 * BLOCK, step).astype(F32)
            reduced = jnp.where(keep, start - product, 0.0).astype(BF16)
            dst[slab, :, :, part] = reduced.reshape(2, BLOCK, step)

    def piv0_of(h, f, owner, to):
        slabs = pl.ds(f * 4, 4)
        return remote(
            parent.at[h, slabs, 0, pl.ds(0, 32), :], piv0.at[h, slabs, owner],
            piv0_send.at[h, f, to], piv0_recv.at[h, f, owner], g * 4 + to, panel,
        )

    def fwd_of(f, half):
        part = pfront.at[pl.ds(f * 4, 4), half]
        return remote(part, part, fwd_send.at[f], fwd_recv.at[f], leaf, mate)

    def open_front(h, f):
        @pl.loop(0, 2)
        def _(j):
            extend(front.at[h], parent.at[h], 0, f * 4 + j, f * 4 + j + 2)

        @pl.loop(1, 4)
        def _(i):
            piv0_of(h, f, r, (r + i) % 4).start()

        @pl.loop(0, 4)
        def _(j):
            piv0[h, f * 4 + j, r] = parent[h, f * 4 + j, 0, 0:32, :]

    def open_stage(h, stage):
        each_peer(stage, lambda dy, dx: a2a_of(h, at(dy, dx), g).wait_recv())
        if stage == 0:
            own_copy(h).wait()
            open_front(h, y)
        elif stage == 1:
            @pl.loop(0, 2)
            def _(i):
                open_front(h, (y + 1 + 2 * i) % 4)
        else:
            open_front(h, (y + 2) % 4)

    def open_panel(f):
        fwd_of(f, 1 - core).wait_recv()

        @pl.loop(0, 2)
        def _(j):
            extend(pfront, pparent0, 0, f * 4 + j, f * 4 + j + 2)

    piece = pl.ds(multiple(x * BLOCK, BLOCK), BLOCK)

    def pp0_of(owner, to):
        return remote(
            pparent0.at[pl.ds(y * 4, 4), 0, pl.ds(0, 32), piece], ppiv0.at[:, owner],
            pp0_send.at[to], pp0_recv.at[owner], g * 4 + to, panel,
        )

    spread_upper0 = Spread(
        lambda slab: pupper0.at[
            slab // 4, pl.ds(multiple(core * 256, 256), 256), pl.ds(multiple(slab % 4 * BLOCK, BLOCK), BLOCK)
        ],
        up0_send, up0_recv,
    )

    def up0f_of(f, half):
        part = pupper0.at[f, pl.ds(multiple(half * 256, 256), 256), :]
        return remote(part, part, up0f_send.at[f], up0f_recv.at[f], leaf, mate)

    def piv1_of(h, owner, to):
        return remote(
            parent.at[h, :, 0, pl.ds(0, 16), :], piv1.at[h, :, owner],
            piv1_send.at[h, to], piv1_recv.at[h, owner], g * 4 + to, panel,
        )

    def pp1_of(owner, to):
        return remote(
            pparent1.at[pl.ds(y // 2 * 8, 8), 0, pl.ds(0, 16), piece], ppiv1.at[:, owner],
            pp1_send.at[to], pp1_recv.at[owner], g * 4 + to, panel,
        )

    spread_upper1 = Spread(
        lambda slab: pupper1.at[
            slab // 8,
            pl.ds(multiple(core * 256 + slab // 4 % 2 * BLOCK, BLOCK), BLOCK),
            pl.ds(multiple(slab % 4 * BLOCK, BLOCK), BLOCK),
        ],
        up1_send, up1_recv,
    )

    def up1f_of(f, half):
        part = pupper1.at[f, pl.ds(multiple(half * 256, 256), 256), :]
        return remote(part, part, up1f_send.at[f], up1f_recv.at[f], leaf, mate)

    def piv2_of(h, owner, to):
        part = piv2.at[h, owner]
        return remote(part, part, piv2_send.at[h, to], piv2_recv.at[h, owner], g * 4 + to, panel)

    def out_of(h, slab, to):
        return remote(
            front.at[h, to], out.at[:, :, columns(slab, h)],
            out_send.at[h, to], out_recv.at[h, slab], to * 4 + r, panel,
        )

    def others(visit):
        @pl.loop(1, 4)
        def _(i):
            visit((r + i) % 4)

    def own_level0(h):
        @pl.loop(0, 4)
        def _(i):
            f = (y + i + i // 2 - 2 * (i // 3)) % 4
            others(lambda owner: piv0_of(h, f, owner, r).wait_recv())
            upper[h, f] = jnp.dot(
                inv[f], piv0[h, pl.ds(f * 4, 4)].reshape(PANEL, HALF), preferred_element_type=F32
            ).astype(BF16)

            @pl.loop(0, 4)
            def _(j):
                subtract(parent.at[h], pparent0, front.at[h], upper.at[h, f], f * 4 + j, 32)

        @pl.loop(0, 4)
        def _(f):
            others(lambda to: piv0_of(h, f, r, to).wait_send())

        @pl.loop(0, 8)
        def _(j):
            a = j + j // 4 * 4
            extend(front.at[h], parent.at[h], 1, a, a + 4)

        others(lambda to: piv1_of(h, r, to).start())

        @pl.loop(0, 16)
        def _(j):
            piv1[h, j, r] = parent[h, j, 0, 0:16, :]

    def own_level1(h):
        others(lambda owner: piv1_of(h, owner, r).wait_recv())

        @pl.loop(0, 2)
        def _(f):
            upper[h, f] = jnp.dot(
                inv[4 + f], piv1[h, pl.ds(f * 8, 8)].reshape(PANEL, HALF), preferred_element_type=F32
            ).astype(BF16)

            @pl.loop(0, 8)
            def _(j):
                subtract(parent.at[h], pparent1, front.at[h], upper.at[h, f], f * 8 + j, 16)

        others(lambda to: piv1_of(h, r, to).wait_send())

        @pl.loop(0, 8)
        def _(j):
            extend(front.at[h], parent.at[h], 2, j, j + 8)

        @pl.loop(0, 8)
        def _(j):
            pair = [parent[h, 2 * j + k, 0, 0:16, :].astype(F32)[0:8] for k in range(2)]
            piv2[h, r, j] = jnp.concatenate(pair, axis=0).astype(BF16)

        others(lambda to: piv2_of(h, r, to).start())

    def own_level2(h):
        others(lambda owner: piv2_of(h, owner, r).wait_recv())

        @pl.loop(0, 4)
        def _(owner):
            @pl.loop(0, 8)
            def _(j):
                both = piv2[h, owner, j].astype(F32)
                piv2_wide[2 * j, owner] = both[0:8]
                piv2_wide[2 * j + 1, owner] = both[8:16]

        upper[h, 0] = jnp.dot(
            inv[6], piv2_wide[...].reshape(PANEL, HALF).astype(BF16), preferred_element_type=F32
        ).astype(BF16)

        def finish(dy, dx):
            to = at(dy, dx)
            subtract(parent.at[h], pparent2, front.at[h], upper.at[h, 0], to, 8)
            out_of(h, g, to).start()

        for stage in range(3):
            each_peer(stage, finish)
        subtract(parent.at[h], pparent2, front.at[h], upper.at[h, 0], g, 8)
        home(h).start()

    def home(h):
        return pltpu.make_async_copy(front.at[h, g], out.at[:, :, columns(g, h)], local_sem.at[4 + h])

    for stage in range(3):
        open_stage(0, stage)
    spread_panel.pass_on()
    send_child(1, 0)
    spread_panel.take_direct()
    fwd_of(y, core).start()
    open_panel(y)
    others(lambda to: pp0_of(r, to).start())

    @pl.loop(0, 4)
    def _(j):
        ppiv0[j, r] = pparent0[y * 4 + j, 0, 0:32, piece]

    inv_copy.wait()
    others(lambda owner: pp0_of(owner, r).wait_recv())
    half0 = pl.ds(multiple(core * 256, 256), 256)
    pupper0[y, half0, piece] = jnp.dot(
        inv[y, half0, :], ppiv0[...].reshape(PANEL, BLOCK), preferred_element_type=F32
    ).astype(BF16)
    spread_upper0.begin()
    send_child(1, 1)
    send_child(1, 2)

    spread_panel.take_passed()

    @pl.loop(1, 4)
    def _(i):
        fwd_of((y + i) % 4, core).start()

    @pl.loop(1, 4)
    def _(i):
        open_panel((y + i) % 4)

    own_level0(0)
    spread_upper0.pass_on()
    open_stage(1, 0)

    spread_upper0.take_direct()
    spread_upper0.take_passed()

    @pl.loop(0, 4)
    def _(f):
        up0f_of(f, core).start()

    @pl.when(panel == 0)
    def _():
        for index in range(3):
            first_copy(0, 1, index).wait_send()

    spread_panel.sent()

    @pl.loop(0, 4)
    def _(f):
        fwd_of(f, core).wait_send()

    @pl.loop(0, 4)
    def _(f):
        up0f_of(f, 1 - core).wait_recv()

        @pl.loop(0, 4)
        def _(j):
            subtract(pparent0, pparent0, pfront, pupper0.at[f], f * 4 + j, 32)

    @pl.loop(0, 8)
    def _(j):
        a = j + j // 4 * 4
        extend(pfront, pparent1, 1, a, a + 4)

    others(lambda to: pp1_of(r, to).start())

    @pl.loop(0, 8)
    def _(j):
        ppiv1[j, r] = pparent1[y // 2 * 8 + j, 0, 0:16, piece]

    open_stage(1, 1)
    open_stage(1, 2)
    own_level1(0)

    others(lambda owner: pp1_of(owner, r).wait_recv())
    quarter = pl.ds(multiple(core * 256 + y % 2 * BLOCK, BLOCK), BLOCK)
    pupper1[y // 2, quarter, piece] = jnp.dot(
        inv[4 + y // 2, quarter, :], ppiv1[...].reshape(PANEL, BLOCK), preferred_element_type=F32
    ).astype(BF16)
    spread_upper1.begin()
    own_level0(1)
    spread_upper1.pass_on()
    spread_upper1.take_direct()
    spread_upper1.take_passed()

    @pl.loop(0, 2)
    def _(f):
        up1f_of(f, core).start()

    @pl.loop(0, 2)
    def _(f):
        up1f_of(f, 1 - core).wait_recv()

        @pl.loop(0, 8)
        def _(j):
            subtract(pparent1, pparent1, pfront, pupper1.at[f], f * 8 + j, 16)

    @pl.loop(0, 8)
    def _(j):
        extend(pfront, pparent2, 2, j, j + 8)

    own_level2(0)
    own_level1(1)
    own_level2(1)

    for h in range(2):
        home(h).wait()

    def settle(dy, dx):
        slab = at(dy, dx)
        map_of(g, slab).wait_send()
        for h in range(2):
            out_of(h, slab, g).wait_recv()
            out_of(h, g, slab).wait_send()
            a2a_of(h, g, slab).wait_send()

    for stage in range(3):
        each_peer(stage, settle)
    spread_upper0.sent()
    spread_upper1.sent()

    @pl.loop(0, 4)
    def _(f):
        up0f_of(f, core).wait_send()

    @pl.loop(0, 2)
    def _(f):
        up1f_of(f, core).wait_send()

    def leave(to):
        pp0_of(r, to).wait_send()
        pp1_of(r, to).wait_send()
        for h in range(2):
            piv2_of(h, r, to).wait_send()

    others(leave)


def on_device(child_front, own_map, cross_map, pivot_inverse):
    rows, width = child_front.shape
    maps = jnp.concatenate([own_map[:, 0, :], cross_map[:, 0, :]], axis=1)
    maps = jnp.pad(maps, ((0, 8 - maps.shape[0]), (0, 128 - maps.shape[1])))
    dma = pltpu.SemaphoreType.DMA
    call = pl.pallas_call(
        kernel,
        out_shape=jax.ShapeDtypeStruct((2, BLOCK, width), BF16),
        in_specs=[
            pl.BlockSpec(memory_space=pl.ANY),
            pl.BlockSpec(memory_space=pltpu.VMEM),
            pl.BlockSpec(memory_space=pl.ANY),
        ],
        out_specs=pl.BlockSpec(memory_space=pl.ANY),
        scratch_shapes=[
            pltpu.VMEM((2, 16, 2, BLOCK, HALF), BF16),
            pltpu.VMEM((2, 16, 2, BLOCK, HALF), BF16),
            pltpu.VMEM((16, 2, BLOCK, PANEL), BF16),
            pltpu.VMEM((16, 2, BLOCK, PANEL), BF16),
            pltpu.VMEM((16, 2, BLOCK, PANEL), BF16),
            pltpu.VMEM((16, 2, BLOCK, PANEL), BF16),
            pltpu.VMEM((7, PANEL, PANEL), BF16),
            pltpu.VMEM((16, 8, 128), jnp.int32),
            pltpu.SMEM((16, 8, 128), jnp.int32),
            pltpu.VMEM((2, 16, 4, 32, HALF), BF16),
            pltpu.VMEM((2, 16, 4, 16, HALF), BF16),
            pltpu.VMEM((2, 4, 8, 16, HALF), BF16),
            pltpu.VMEM((16, 4, 8, HALF), F32),
            pltpu.VMEM((4, 4, 32, BLOCK), BF16),
            pltpu.VMEM((8, 4, 16, BLOCK), BF16),
            pltpu.VMEM((2, 4, PANEL, HALF), BF16),
            pltpu.VMEM((4, PANEL, PANEL), BF16),
            pltpu.VMEM((2, PANEL, PANEL), BF16),
            dma((16,)), dma((16,)), dma((2, 16)), dma((2, 16)), dma((3,)), dma((1,)),
            dma((4, 4)), dma((16,)), dma((4,)), dma((4,)), dma((2, 4, 4)), dma((2, 4, 4)),
            dma((2, 4)), dma((2, 4)), dma((2, 4)), dma((2, 4)), dma((4,)), dma((4,)),
            dma((4,)), dma((4,)), dma((4, 4)), dma((16,)), dma((4,)), dma((4,)),
            dma((4, 4)), dma((16,)), dma((2,)), dma((2,)), dma((2, 16)), dma((2, 16)), dma((6,)),
        ],
        compiler_params=pltpu.CompilerParams(
            collective_id=0, has_side_effects=True, vmem_limit_bytes=60 * 1024 * 1024
        ),
        cost_estimate=pl.CostEstimate(
            flops=9_000_000_000, bytes_accessed=16_000_000, transcendentals=0
        ),
    )
    result = call(child_front.reshape(2, BLOCK, width), maps, pivot_inverse)
    return result.reshape(rows, width)


def solution(mesh):
    placed = (P("leaf", "panel"), P(None, "leaf", None), P(None, "leaf", None), P())
    return jax.shard_map(
        on_device, mesh=mesh, in_specs=placed, out_specs=P("leaf", "panel"), check_vma=False
    )
```

```python
import functools

import jax
import jax.numpy as jnp
from jax import lax
from jax.experimental import pallas as pl
from jax.experimental.pallas import tpu as pltpu
from jax.sharding import PartitionSpec as P

PANEL = 512
BLOCK = 128
WIDTH = 256
HALF = 128
MESH = pl.DeviceIdType.MESH
F32 = jnp.float32
BF16 = jnp.bfloat16


def multiple(value, of):
    return pl.multiple_of(value, of)


def kernel(
    child, maps, inverse, out,
    front, parent, pfront, pparent0, pparent1, pparent2, inv, map_buf, map_tab,
    piv0, piv1, piv2, piv2_wide, ppiv0, ppiv1, upper, pupper0, pupper1,
    map_send, map_recv, a2a_send, a2a_recv, first_send, first_recv,
    pan_send, pan_recv, fwd_send, fwd_recv, piv0_send, piv0_recv,
    piv1_send, piv1_recv, piv2_send, piv2_recv, pp0_send, pp0_recv,
    pp1_send, pp1_recv, up0_send, up0_recv, up0f_send, up0f_recv,
    up1_send, up1_recv, up1f_send, up1f_recv, out_send, out_recv, local_sem,
):
    leaf = lax.axis_index("leaf")
    panel = lax.axis_index("panel")
    g, r = leaf // 4, leaf % 4
    y, x = g // 4, g % 4
    core = panel % 2
    mate = panel + 1 - 2 * core

    def at(dy, dx):
        return ((y + dy) % 4) * 4 + (x + dx) % 4

    def each_peer(stage, visit):
        if stage == 0:
            @pl.loop(1, 4)
            def _(i):
                visit(0, i)
        elif stage == 1:
            @pl.loop(0, 4)
            def _(i):
                visit(1, i)
                visit(3, i)
        else:
            @pl.loop(0, 4)
            def _(i):
                visit(2, i)

    def remote(src, dst, send, recv, to_leaf, to_panel):
        return pltpu.make_async_remote_copy(
            src_ref=src, dst_ref=dst, send_sem=send, recv_sem=recv,
            device_id=(to_leaf, to_panel), device_id_type=MESH,
        )

    def crossed(first, second):
        return at(core * first + (1 - core) * second, core * second + (1 - core) * first)

    class Spread:
        def __init__(self, part_of, send, recv):
            self.part_of, self.send, self.recv = part_of, send, recv

        def copy(self, slab, i, j, to):
            part = self.part_of(slab)
            return remote(part, part, self.send.at[i, j], self.recv.at[slab], to * 4 + r, panel)

        def begin(self):
            @pl.loop(1, 4)
            def _(i):
                self.copy(g, i, 0, crossed(i, 0)).start()
                self.copy(g, 0, i, crossed(0, i)).start()

        def pass_on(self):
            @pl.loop(1, 4)
            def _(i):
                slab = crossed(i, 0)
                self.copy(slab, 0, 0, g).wait_recv()

                @pl.loop(1, 4)
                def _(j):
                    self.copy(slab, i, j, crossed(0, j)).start()

        def take_direct(self):
            @pl.loop(1, 4)
            def _(j):
                self.copy(crossed(0, j), 0, 0, g).wait_recv()

        def take_passed(self):
            @pl.loop(1, 4)
            def _(i):
                @pl.loop(1, 4)
                def _(j):
                    self.copy(crossed(i, j), 0, 0, g).wait_recv()

        def sent(self):
            @pl.loop(1, 4)
            def _(i):
                self.copy(g, i, 0, crossed(i, 0)).wait_send()
                self.copy(g, 0, i, crossed(0, i)).wait_send()

                @pl.loop(1, 4)
                def _(j):
                    self.copy(crossed(i, 0), i, j, crossed(0, j)).wait_send()

    barrier = pltpu.get_barrier_semaphore()

    def greet(dy, dx):
        pl.semaphore_signal(barrier, inc=1, device_id=(at(dy, dx) * 4 + r, panel), device_id_type=MESH)

    for stage in range(3):
        each_peer(stage, greet)

    @pl.loop(1, 4)
    def _(i):
        pl.semaphore_signal(barrier, inc=1, device_id=(g * 4 + (r + i) % 4, panel), device_id_type=MESH)
        pl.semaphore_signal(barrier, inc=1, device_id=(leaf, (panel + i) % 4), device_id_type=MESH)

    def columns(which, h):
        return pl.ds(multiple(which * WIDTH + h * HALF, HALF), HALF)

    def own_copy(h):
        return pltpu.make_async_copy(child.at[:, :, columns(g, h)], front.at[h, g], local_sem.at[4 + h])

    own_copy(0).start()
    own_copy(1).start()
    inv_copy = pltpu.make_async_copy(inverse, inv, local_sem.at[1])
    inv_copy.start()
    map_copy = pltpu.make_async_copy(maps, map_buf.at[g], local_sem.at[2])
    map_copy.start()
    pl.semaphore_wait(barrier, 21)

    def first_copy(half, to_panel, index):
        return remote(
            child.at[half, :, pl.ds(0, PANEL)], pfront.at[g, half],
            first_send.at[index], first_recv.at[0], leaf, to_panel,
        )

    first_own = pltpu.make_async_copy(child.at[0, :, pl.ds(0, PANEL)], pfront.at[g, 0], local_sem.at[3])

    @pl.when(panel == 0)
    def _():
        first_copy(0, 2, 1).start()
        first_copy(1, 3, 2).start()
        first_copy(1, 1, 0).start()
        first_own.start()

    def map_of(slab, to):
        return remote(maps, map_buf.at[slab], map_send.at[to], map_recv.at[slab], to * 4 + r, panel)

    def a2a_of(h, slab, to):
        return remote(
            child.at[:, :, columns(to, h)], front.at[h, slab],
            a2a_send.at[h, to], a2a_recv.at[h, slab], to * 4 + r, panel,
        )

    spread_panel = Spread(lambda slab: pfront.at[slab, core], pan_send, pan_recv)

    def send_child(h, stage):
        each_peer(stage, lambda dy, dx: a2a_of(h, g, at(dy, dx)).start())

    for stage in range(3):
        each_peer(stage, lambda dy, dx: map_of(g, at(dy, dx)).start())
    for stage in range(3):
        send_child(0, stage)

    @pl.when(panel == 0)
    def _():
        first_own.wait()

    @pl.when(panel != 0)
    def _():
        first_copy(core, panel, 0).wait_recv()

    spread_panel.begin()

    map_copy.wait()

    def take_map(dy, dx):
        map_of(at(dy, dx), g).wait_recv()

    for stage in range(3):
        each_peer(stage, take_map)
    to_smem = pltpu.make_async_copy(map_buf, map_tab, local_sem.at[2])
    to_smem.start()
    to_smem.wait()

    def extend(src, dst, level, a, b):
        width = src.shape[3]
        step = min(width, WIDTH)
        for mine, other in ((a, b), (b, a)):
            for slot in range(2):
                from_own = map_tab[mine, level, slot] == 0
                from_cross = map_tab[mine, level, 2 + slot] == 0

                @pl.loop(0, BLOCK // 32)
                def _(q):
                    for left in range(0, width, step):
                        part = (pl.ds(multiple(q * 32, 32), 32), pl.ds(left, step))
                        kept = jnp.where(from_own, src[(mine, 0) + part], src[(mine, 1) + part])
                        moved = jnp.where(from_cross, src[(other, 0) + part], src[(other, 1) + part])
                        dst[(mine, slot) + part] = (kept.astype(F32) + moved.astype(F32)).astype(BF16)

    def subtract(src, columns_of, dst, factor, slab, rows, count=2):
        width = src.shape[3]
        step = min(width, WIDTH)
        slabs = pl.ds(slab, count)
        left = columns_of[slabs].reshape(count * 2 * BLOCK, PANEL)
        for low in range(0, width, step):
            part = pl.ds(low, step)
            product = jnp.dot(left, factor[:, part], preferred_element_type=F32)
            start = src[slabs, :, :, part].reshape(count * 2 * BLOCK, step).astype(F32)
            dst[slabs, :, :, part] = (start - product).astype(BF16).reshape(count, 2, BLOCK, step)
        for k in range(count):
            if rows % 16:
                keep = lax.broadcasted_iota(jnp.int32, (16, width), 0) >= rows
                top = dst[slab + k, 0, 0:16, :].astype(F32)
                dst[slab + k, 0, 0:16, :] = jnp.where(keep, top, 0.0).astype(BF16)
            else:
                dst[slab + k, 0, 0:rows, :] = jnp.zeros((rows, width), BF16)

    def piv0_of(h, f, owner, to):
        slabs = pl.ds(f * 4, 4)
        return remote(
            parent.at[h, slabs, 0, pl.ds(0, 32), :], piv0.at[h, slabs, owner],
            piv0_send.at[h, f, to], piv0_recv.at[h, f, owner], g * 4 + to, panel,
        )

    def fwd_of(f, half):
        part = pfront.at[pl.ds(f * 4, 4), half]
        return remote(part, part, fwd_send.at[f], fwd_recv.at[f], leaf, mate)

    def open_front(h, f):
        @pl.loop(0, 2)
        def _(j):
            extend(front.at[h], parent.at[h], 0, f * 4 + j, f * 4 + j + 2)

        @pl.loop(1, 4)
        def _(i):
            piv0_of(h, f, r, (r + i) % 4).start()

        @pl.loop(0, 4)
        def _(j):
            piv0[h, f * 4 + j, r] = parent[h, f * 4 + j, 0, 0:32, :]

    def open_stage(h, stage):
        each_peer(stage, lambda dy, dx: a2a_of(h, at(dy, dx), g).wait_recv())
        if stage == 0:
            own_copy(h).wait()
            open_front(h, y)
        elif stage == 1:
            @pl.loop(0, 2)
            def _(i):
                open_front(h, (y + 1 + 2 * i) % 4)
        else:
            open_front(h, (y + 2) % 4)

    def open_panel(f):
        fwd_of(f, 1 - core).wait_recv()

        @pl.loop(0, 2)
        def _(j):
            extend(pfront, pparent0, 0, f * 4 + j, f * 4 + j + 2)

    piece = pl.ds(multiple(x * BLOCK, BLOCK), BLOCK)

    def pp0_of(owner, to):
        return remote(
            pparent0.at[pl.ds(y * 4, 4), 0, pl.ds(0, 32), piece], ppiv0.at[:, owner],
            pp0_send.at[to], pp0_recv.at[owner], g * 4 + to, panel,
        )

    spread_upper0 = Spread(
        lambda slab: pupper0.at[
            slab // 4, pl.ds(multiple(core * 256, 256), 256), pl.ds(multiple(slab % 4 * BLOCK, BLOCK), BLOCK)
        ],
        up0_send, up0_recv,
    )

    def up0f_of(f, half):
        part = pupper0.at[f, pl.ds(multiple(half * 256, 256), 256), :]
        return remote(part, part, up0f_send.at[f], up0f_recv.at[f], leaf, mate)

    def piv1_of(h, owner, to):
        return remote(
            parent.at[h, :, 0, pl.ds(0, 16), :], piv1.at[h, :, owner],
            piv1_send.at[h, to], piv1_recv.at[h, owner], g * 4 + to, panel,
        )

    def pp1_of(owner, to):
        return remote(
            pparent1.at[pl.ds(y // 2 * 8, 8), 0, pl.ds(0, 16), piece], ppiv1.at[:, owner],
            pp1_send.at[to], pp1_recv.at[owner], g * 4 + to, panel,
        )

    spread_upper1 = Spread(
        lambda slab: pupper1.at[
            slab // 8,
            pl.ds(multiple(core * 256 + slab // 4 % 2 * BLOCK, BLOCK), BLOCK),
            pl.ds(multiple(slab % 4 * BLOCK, BLOCK), BLOCK),
        ],
        up1_send, up1_recv,
    )

    def up1f_of(f, half):
        part = pupper1.at[f, pl.ds(multiple(half * 256, 256), 256), :]
        return remote(part, part, up1f_send.at[f], up1f_recv.at[f], leaf, mate)

    def piv2_of(h, owner, to):
        part = piv2.at[h, owner]
        return remote(part, part, piv2_send.at[h, to], piv2_recv.at[h, owner], g * 4 + to, panel)

    def out_of(h, slab, to):
        return remote(
            front.at[h, to], out.at[:, :, columns(slab, h)],
            out_send.at[h, to], out_recv.at[h, slab], to * 4 + r, panel,
        )

    def others(visit):
        @pl.loop(1, 4)
        def _(i):
            visit((r + i) % 4)

    def own_level0(h):
        @pl.loop(0, 4)
        def _(i):
            f = (y + i + i // 2 - 2 * (i // 3)) % 4
            others(lambda owner: piv0_of(h, f, owner, r).wait_recv())
            upper[h, f] = jnp.dot(
                inv[f], piv0[h, pl.ds(f * 4, 4)].reshape(PANEL, HALF), preferred_element_type=F32
            ).astype(BF16)

            subtract(parent.at[h], pparent0, front.at[h], upper.at[h, f], f * 4, 32, 4)

        @pl.loop(0, 4)
        def _(f):
            others(lambda to: piv0_of(h, f, r, to).wait_send())

        @pl.loop(0, 8)
        def _(j):
            a = j + j // 4 * 4
            extend(front.at[h], parent.at[h], 1, a, a + 4)

        others(lambda to: piv1_of(h, r, to).start())

        @pl.loop(0, 16)
        def _(j):
            piv1[h, j, r] = parent[h, j, 0, 0:16, :]

    def own_level1(h):
        others(lambda owner: piv1_of(h, owner, r).wait_recv())

        @pl.loop(0, 2)
        def _(f):
            upper[h, f] = jnp.dot(
                inv[4 + f], piv1[h, pl.ds(f * 8, 8)].reshape(PANEL, HALF), preferred_element_type=F32
            ).astype(BF16)

            @pl.loop(0, 2)
            def _(j):
                subtract(parent.at[h], pparent1, front.at[h], upper.at[h, f], f * 8 + j * 4, 16, 4)

        others(lambda to: piv1_of(h, r, to).wait_send())

        @pl.loop(0, 8)
        def _(j):
            extend(front.at[h], parent.at[h], 2, j, j + 8)

        @pl.loop(0, 8)
        def _(j):
            pair = [parent[h, 2 * j + k, 0, 0:16, :].astype(F32)[0:8] for k in range(2)]
            piv2[h, r, j] = jnp.concatenate(pair, axis=0).astype(BF16)

        others(lambda to: piv2_of(h, r, to).start())

    def own_level2(h):
        others(lambda owner: piv2_of(h, owner, r).wait_recv())

        @pl.loop(0, 4)
        def _(owner):
            @pl.loop(0, 8)
            def _(j):
                both = piv2[h, owner, j].astype(F32)
                piv2_wide[2 * j, owner] = both[0:8]
                piv2_wide[2 * j + 1, owner] = both[8:16]

        upper[h, 0] = jnp.dot(
            inv[6], piv2_wide[...].reshape(PANEL, HALF).astype(BF16), preferred_element_type=F32
        ).astype(BF16)

        def finish(dy, dx):
            to = at(dy, dx)
            subtract(parent.at[h], pparent2, front.at[h], upper.at[h, 0], to, 8, 1)
            out_of(h, g, to).start()

        for stage in range(3):
            each_peer(stage, finish)
        subtract(parent.at[h], pparent2, front.at[h], upper.at[h, 0], g, 8, 1)
        home(h).start()

    def home(h):
        return pltpu.make_async_copy(front.at[h, g], out.at[:, :, columns(g, h)], local_sem.at[4 + h])

    for stage in range(3):
        open_stage(0, stage)
    spread_panel.pass_on()
    send_child(1, 0)
    spread_panel.take_direct()
    fwd_of(y, core).start()
    open_panel(y)
    others(lambda to: pp0_of(r, to).start())

    @pl.loop(0, 4)
    def _(j):
        ppiv0[j, r] = pparent0[y * 4 + j, 0, 0:32, piece]

    send_child(1, 1)
    inv_copy.wait()
    others(lambda owner: pp0_of(owner, r).wait_recv())
    half0 = pl.ds(multiple(core * 256, 256), 256)
    pupper0[y, half0, piece] = jnp.dot(
        inv[y, half0, :], ppiv0[...].reshape(PANEL, BLOCK), preferred_element_type=F32
    ).astype(BF16)
    spread_upper0.begin()
    spread_panel.take_passed()

    @pl.loop(1, 4)
    def _(i):
        fwd_of((y + i) % 4, core).start()

    spread_upper0.pass_on()
    send_child(1, 2)

    @pl.loop(1, 4)
    def _(i):
        open_panel((y + i) % 4)

    own_level0(0)

    spread_upper0.take_direct()
    spread_upper0.take_passed()

    @pl.loop(0, 4)
    def _(f):
        up0f_of(f, core).start()

    @pl.when(panel == 0)
    def _():
        for index in range(3):
            first_copy(0, 1, index).wait_send()

    spread_panel.sent()

    @pl.loop(0, 4)
    def _(f):
        fwd_of(f, core).wait_send()

    @pl.loop(0, 4)
    def _(f):
        up0f_of(f, 1 - core).wait_recv()

        @pl.loop(0, 2)
        def _(j):
            subtract(pparent0, pparent0, pfront, pupper0.at[f], f * 4 + j * 2, 32)

    @pl.loop(0, 8)
    def _(j):
        a = j + j // 4 * 4
        extend(pfront, pparent1, 1, a, a + 4)

    others(lambda to: pp1_of(r, to).start())

    @pl.loop(0, 8)
    def _(j):
        ppiv1[j, r] = pparent1[y // 2 * 8 + j, 0, 0:16, piece]

    open_stage(1, 0)
    open_stage(1, 1)
    own_level1(0)

    others(lambda owner: pp1_of(owner, r).wait_recv())
    quarter = pl.ds(multiple(core * 256 + y % 2 * BLOCK, BLOCK), BLOCK)
    pupper1[y // 2, quarter, piece] = jnp.dot(
        inv[4 + y // 2, quarter, :], ppiv1[...].reshape(PANEL, BLOCK), preferred_element_type=F32
    ).astype(BF16)
    spread_upper1.begin()
    open_stage(1, 2)
    spread_upper1.pass_on()
    own_level0(1)
    spread_upper1.take_direct()
    spread_upper1.take_passed()

    @pl.loop(0, 2)
    def _(f):
        up1f_of(f, core).start()

    @pl.loop(0, 2)
    def _(f):
        up1f_of(f, 1 - core).wait_recv()

        @pl.loop(0, 4)
        def _(j):
            subtract(pparent1, pparent1, pfront, pupper1.at[f], f * 8 + j * 2, 16)

    @pl.loop(0, 8)
    def _(j):
        extend(pfront, pparent2, 2, j, j + 8)

    own_level2(0)
    own_level1(1)
    own_level2(1)

    for h in range(2):
        home(h).wait()

    def settle(dy, dx):
        slab = at(dy, dx)
        map_of(g, slab).wait_send()
        for h in range(2):
            out_of(h, slab, g).wait_recv()
            out_of(h, g, slab).wait_send()
            a2a_of(h, g, slab).wait_send()

    for stage in range(3):
        each_peer(stage, settle)
    spread_upper0.sent()
    spread_upper1.sent()

    @pl.loop(0, 4)
    def _(f):
        up0f_of(f, core).wait_send()

    @pl.loop(0, 2)
    def _(f):
        up1f_of(f, core).wait_send()

    def leave(to):
        pp0_of(r, to).wait_send()
        pp1_of(r, to).wait_send()
        for h in range(2):
            piv2_of(h, r, to).wait_send()

    others(leave)


def on_device(child_front, own_map, cross_map, pivot_inverse):
    rows, width = child_front.shape
    maps = jnp.concatenate([own_map[:, 0, :], cross_map[:, 0, :]], axis=1)
    maps = jnp.pad(maps, ((0, 8 - maps.shape[0]), (0, 128 - maps.shape[1])))
    dma = pltpu.SemaphoreType.DMA
    call = pl.pallas_call(
        kernel,
        out_shape=jax.ShapeDtypeStruct((2, BLOCK, width), BF16),
        in_specs=[
            pl.BlockSpec(memory_space=pl.ANY),
            pl.BlockSpec(memory_space=pltpu.VMEM),
            pl.BlockSpec(memory_space=pl.ANY),
        ],
        out_specs=pl.BlockSpec(memory_space=pl.ANY),
        scratch_shapes=[
            pltpu.VMEM((2, 16, 2, BLOCK, HALF), BF16),
            pltpu.VMEM((2, 16, 2, BLOCK, HALF), BF16),
            pltpu.VMEM((16, 2, BLOCK, PANEL), BF16),
            pltpu.VMEM((16, 2, BLOCK, PANEL), BF16),
            pltpu.VMEM((16, 2, BLOCK, PANEL), BF16),
            pltpu.VMEM((16, 2, BLOCK, PANEL), BF16),
            pltpu.VMEM((7, PANEL, PANEL), BF16),
            pltpu.VMEM((16, 8, 128), jnp.int32),
            pltpu.SMEM((16, 8, 128), jnp.int32),
            pltpu.VMEM((2, 16, 4, 32, HALF), BF16),
            pltpu.VMEM((2, 16, 4, 16, HALF), BF16),
            pltpu.VMEM((2, 4, 8, 16, HALF), BF16),
            pltpu.VMEM((16, 4, 8, HALF), F32),
            pltpu.VMEM((4, 4, 32, BLOCK), BF16),
            pltpu.VMEM((8, 4, 16, BLOCK), BF16),
            pltpu.VMEM((2, 4, PANEL, HALF), BF16),
            pltpu.VMEM((4, PANEL, PANEL), BF16),
            pltpu.VMEM((2, PANEL, PANEL), BF16),
            dma((16,)), dma((16,)), dma((2, 16)), dma((2, 16)), dma((3,)), dma((1,)),
            dma((4, 4)), dma((16,)), dma((4,)), dma((4,)), dma((2, 4, 4)), dma((2, 4, 4)),
            dma((2, 4)), dma((2, 4)), dma((2, 4)), dma((2, 4)), dma((4,)), dma((4,)),
            dma((4,)), dma((4,)), dma((4, 4)), dma((16,)), dma((4,)), dma((4,)),
            dma((4, 4)), dma((16,)), dma((2,)), dma((2,)), dma((2, 16)), dma((2, 16)), dma((6,)),
        ],
        compiler_params=pltpu.CompilerParams(
            collective_id=0, has_side_effects=True, vmem_limit_bytes=60 * 1024 * 1024
        ),
        cost_estimate=pl.CostEstimate(
            flops=9_000_000_000, bytes_accessed=16_000_000, transcendentals=0
        ),
    )
    result = call(child_front.reshape(2, BLOCK, width), maps, pivot_inverse)
    return result.reshape(rows, width)


def solution(mesh):
    placed = (P("leaf", "panel"), P(None, "leaf", None), P(None, "leaf", None), P())
    return jax.shard_map(
        on_device, mesh=mesh, in_specs=placed, out_specs=P("leaf", "panel"), check_vma=False
    )
```

```python
import functools

import jax
import jax.numpy as jnp
from jax import lax
from jax.experimental import pallas as pl
from jax.experimental.pallas import tpu as pltpu
from jax.sharding import PartitionSpec as P

PANEL = 512
BLOCK = 128
WIDTH = 256
HALF = 128
MESH = pl.DeviceIdType.MESH
F32 = jnp.float32
BF16 = jnp.bfloat16


def multiple(value, of):
    return pl.multiple_of(value, of)


def kernel(
    child, own_map, cross_map, inverse, out,
    front, parent, pfront, pparent0, pparent1, pparent2, inv, map_buf, map_tab,
    piv0, piv1, piv2, piv2_wide, ppiv0, ppiv1, upper, pupper0, pupper1,
    map_send, map_recv, a2a_send, a2a_recv, first_send, first_recv,
    pan_send, pan_recv, fwd_send, fwd_recv, piv0_send, piv0_recv,
    piv1_send, piv1_recv, piv2_send, piv2_recv, pp0_send, pp0_recv,
    pp1_send, pp1_recv, up0_send, up0_recv, up0f_send, up0f_recv,
    up1_send, up1_recv, up1f_send, up1f_recv, out_send, out_recv, local_sem,
):
    leaf = lax.axis_index("leaf")
    panel = lax.axis_index("panel")
    g, r = leaf // 4, leaf % 4
    y, x = g // 4, g % 4
    core = panel % 2
    mate = panel + 1 - 2 * core

    def at(dy, dx):
        return ((y + dy) % 4) * 4 + (x + dx) % 4

    def each_peer(stage, visit):
        if stage == 0:
            @pl.loop(1, 4)
            def _(i):
                visit(0, i)
        elif stage == 1:
            @pl.loop(0, 4)
            def _(i):
                visit(1, i)
                visit(3, i)
        else:
            @pl.loop(0, 4)
            def _(i):
                visit(2, i)

    def remote(src, dst, send, recv, to_leaf, to_panel):
        return pltpu.make_async_remote_copy(
            src_ref=src, dst_ref=dst, send_sem=send, recv_sem=recv,
            device_id=(to_leaf, to_panel), device_id_type=MESH,
        )

    def crossed(first, second):
        return at(core * first + (1 - core) * second, core * second + (1 - core) * first)

    class Spread:
        def __init__(self, part_of, send, recv):
            self.part_of, self.send, self.recv = part_of, send, recv

        def copy(self, slab, i, j, to):
            part = self.part_of(slab)
            return remote(part, part, self.send.at[i, j], self.recv.at[slab], to * 4 + r, panel)

        def begin(self):
            @pl.loop(1, 4)
            def _(i):
                self.copy(g, i, 0, crossed(i, 0)).start()
                self.copy(g, 0, i, crossed(0, i)).start()

        def pass_on(self):
            @pl.loop(1, 4)
            def _(i):
                slab = crossed(i, 0)
                self.copy(slab, 0, 0, g).wait_recv()

                @pl.loop(1, 4)
                def _(j):
                    self.copy(slab, i, j, crossed(0, j)).start()

        def take_direct(self):
            @pl.loop(1, 4)
            def _(j):
                self.copy(crossed(0, j), 0, 0, g).wait_recv()

        def take_row(self, dy):
            @pl.loop(1, 4)
            def _(i):
                self.copy(at(dy, i), 0, 0, g).wait_recv()

        def take_passed(self):
            @pl.loop(1, 4)
            def _(i):
                @pl.loop(1, 4)
                def _(j):
                    self.copy(crossed(i, j), 0, 0, g).wait_recv()

        def sent(self):
            @pl.loop(1, 4)
            def _(i):
                self.copy(g, i, 0, crossed(i, 0)).wait_send()
                self.copy(g, 0, i, crossed(0, i)).wait_send()

                @pl.loop(1, 4)
                def _(j):
                    self.copy(crossed(i, 0), i, j, crossed(0, j)).wait_send()

    barrier = pltpu.get_barrier_semaphore()

    def greet(dy, dx):
        pl.semaphore_signal(barrier, inc=1, device_id=(at(dy, dx) * 4 + r, panel), device_id_type=MESH)

    @pl.loop(1, 4)
    def _(i):
        pl.semaphore_signal(barrier, inc=1, device_id=(leaf, (panel + i) % 4), device_id_type=MESH)

    for stage in (2, 1, 0):
        each_peer(stage, greet)

    @pl.loop(1, 4)
    def _(i):
        pl.semaphore_signal(barrier, inc=1, device_id=(g * 4 + (r + i) % 4, panel), device_id_type=MESH)

    def columns(which, h):
        return pl.ds(multiple(which * WIDTH + h * HALF, HALF), HALF)

    def own_copy(h):
        return pltpu.make_async_copy(child.at[:, :, columns(g, h)], front.at[h, g], local_sem.at[4 + h])

    own_copy(0).start()
    own_copy(1).start()
    inv_copy = pltpu.make_async_copy(inverse, inv, local_sem.at[1])
    inv_copy.start()
    row = lax.broadcasted_iota(jnp.int32, (8, 128), 0)
    lane = lax.broadcasted_iota(jnp.int32, (8, 128), 1)
    table = jnp.zeros((8, 128), jnp.int32)
    for level in range(3):
        for slot in range(2):
            table = jnp.where((row == level) & (lane == slot), own_map[slot, level], table)
            table = jnp.where((row == level) & (lane == 2 + slot), cross_map[slot, level], table)
    map_buf[g] = table
    pl.semaphore_wait(barrier, 21)

    def first_copy(half, to_panel, index):
        return remote(
            child.at[half, :, pl.ds(0, PANEL)], pfront.at[g, half],
            first_send.at[index], first_recv.at[0], leaf, to_panel,
        )

    first_own = pltpu.make_async_copy(child.at[0, :, pl.ds(0, PANEL)], pfront.at[g, 0], local_sem.at[3])

    @pl.when(panel == 0)
    def _():
        first_copy(0, 2, 1).start()
        first_copy(1, 3, 2).start()
        first_copy(1, 1, 0).start()
        first_own.start()

    def map_of(slab, to):
        return remote(map_buf.at[slab], map_buf.at[slab], map_send.at[to], map_recv.at[slab], to * 4 + r, panel)

    def a2a_of(h, slab, to):
        return remote(
            child.at[:, :, columns(to, h)], front.at[h, slab],
            a2a_send.at[h, to], a2a_recv.at[h, slab], to * 4 + r, panel,
        )

    spread_panel = Spread(lambda slab: pfront.at[slab, core], pan_send, pan_recv)

    def send_child(h, stage):
        each_peer(stage, lambda dy, dx: a2a_of(h, g, at(dy, dx)).start())

    for stage in range(3):
        each_peer(stage, lambda dy, dx: map_of(g, at(dy, dx)).start())
    for stage in range(3):
        send_child(0, stage)

    @pl.when(panel == 0)
    def _():
        first_own.wait()

    @pl.when(panel != 0)
    def _():
        first_copy(core, panel, 0).wait_recv()

    spread_panel.begin()


    def take_map(dy, dx):
        map_of(at(dy, dx), g).wait_recv()

    for stage in range(3):
        each_peer(stage, take_map)
    to_smem = pltpu.make_async_copy(map_buf, map_tab, local_sem.at[2])
    to_smem.start()
    to_smem.wait()

    def extend(src, dst, level, a, b):
        width = src.shape[3]
        step = min(width, WIDTH)
        for mine, other in ((a, b), (b, a)):
            for slot in range(2):
                own_block = map_tab[mine, level, slot]
                cross_block = map_tab[mine, level, 2 + slot]

                @pl.loop(0, BLOCK // 32)
                def _(q):
                    for left in range(0, width, step):
                        part = (pl.ds(multiple(q * 32, 32), 32), pl.ds(left, step))
                        if level and width == PANEL:
                            kept, moved = src[(mine, own_block) + part], src[(other, cross_block) + part]
                        else:
                            kept = jnp.where(own_block == 0, src[(mine, 0) + part], src[(mine, 1) + part])
                            moved = jnp.where(cross_block == 0, src[(other, 0) + part], src[(other, 1) + part])
                        dst[(mine, slot) + part] = (kept.astype(F32) + moved.astype(F32)).astype(BF16)

    def subtract(src, columns_of, dst, factor, slab, rows, count=2):
        width = src.shape[3]
        step = min(width, WIDTH)
        slabs = pl.ds(slab, count)
        left = columns_of[slabs].reshape(count * 2 * BLOCK, PANEL)
        for low in range(0, width, step):
            part = pl.ds(low, step)
            product = jnp.dot(left, factor[:, part], preferred_element_type=F32)
            start = src[slabs, :, :, part].reshape(count * 2 * BLOCK, step).astype(F32)
            dst[slabs, :, :, part] = (start - product).astype(BF16).reshape(count, 2, BLOCK, step)
        for k in range(count):
            if rows % 16:
                keep = lax.broadcasted_iota(jnp.int32, (16, width), 0) >= rows
                top = dst[slab + k, 0, 0:16, :].astype(F32)
                dst[slab + k, 0, 0:16, :] = jnp.where(keep, top, 0.0).astype(BF16)
            else:
                dst[slab + k, 0, 0:rows, :] = jnp.zeros((rows, width), BF16)

    def piv0_of(h, f, owner, to):
        slabs = pl.ds(f * 4, 4)
        return remote(
            parent.at[h, slabs, 0, pl.ds(0, 32), :], piv0.at[h, slabs, owner],
            piv0_send.at[h, f, to], piv0_recv.at[h, f, owner], g * 4 + to, panel,
        )

    def fwd_of(f, half):
        part = pfront.at[pl.ds(f * 4, 4), half]
        return remote(part, part, fwd_send.at[f], fwd_recv.at[f], leaf, mate)

    def open_front(h, f):
        @pl.loop(0, 2)
        def _(j):
            extend(front.at[h], parent.at[h], 0, f * 4 + j, f * 4 + j + 2)

        @pl.loop(1, 4)
        def _(i):
            piv0_of(h, f, r, (r + i) % 4).start()

        @pl.loop(0, 4)
        def _(j):
            piv0[h, f * 4 + j, r] = parent[h, f * 4 + j, 0, 0:32, :]

    def open_stage(h, stage):
        each_peer(stage, lambda dy, dx: a2a_of(h, at(dy, dx), g).wait_recv())
        if stage == 0:
            own_copy(h).wait()
            open_front(h, y)
        elif stage == 1:
            @pl.loop(0, 2)
            def _(i):
                open_front(h, (y + 1 + 2 * i) % 4)
        else:
            open_front(h, (y + 2) % 4)

    def open_panel(f):
        fwd_of(f, 1 - core).wait_recv()

        @pl.loop(0, 2)
        def _(j):
            extend(pfront, pparent0, 0, f * 4 + j, f * 4 + j + 2)

    piece = pl.ds(multiple(x * BLOCK, BLOCK), BLOCK)

    def pp0_of(owner, to):
        return remote(
            pparent0.at[pl.ds(y * 4, 4), 0, pl.ds(0, 32), piece], ppiv0.at[:, owner],
            pp0_send.at[to], pp0_recv.at[owner], g * 4 + to, panel,
        )

    spread_upper0 = Spread(
        lambda slab: pupper0.at[
            slab // 4, pl.ds(multiple(core * 256, 256), 256), pl.ds(multiple(slab % 4 * BLOCK, BLOCK), BLOCK)
        ],
        up0_send, up0_recv,
    )

    def up0f_of(f, half):
        part = pupper0.at[f, pl.ds(multiple(half * 256, 256), 256), :]
        return remote(part, part, up0f_send.at[f], up0f_recv.at[f], leaf, mate)

    def piv1_of(h, owner, to):
        return remote(
            parent.at[h, :, 0, pl.ds(0, 16), :], piv1.at[h, :, owner],
            piv1_send.at[h, to], piv1_recv.at[h, owner], g * 4 + to, panel,
        )

    def pp1_of(owner, to):
        return remote(
            pparent1.at[pl.ds(y // 2 * 8, 8), 0, pl.ds(0, 16), piece], ppiv1.at[:, owner],
            pp1_send.at[to], pp1_recv.at[owner], g * 4 + to, panel,
        )

    spread_upper1 = Spread(
        lambda slab: pupper1.at[
            slab // 8,
            pl.ds(multiple(core * 256 + slab // 4 % 2 * BLOCK, BLOCK), BLOCK),
            pl.ds(multiple(slab % 4 * BLOCK, BLOCK), BLOCK),
        ],
        up1_send, up1_recv,
    )

    def up1f_of(f, half):
        part = pupper1.at[f, pl.ds(multiple(half * 256, 256), 256), :]
        return remote(part, part, up1f_send.at[f], up1f_recv.at[f], leaf, mate)

    def piv2_of(h, owner, to):
        part = piv2.at[h, owner]
        return remote(part, part, piv2_send.at[h, to], piv2_recv.at[h, owner], g * 4 + to, panel)

    def out_of(h, slab, to):
        return remote(
            front.at[h, to], out.at[:, :, columns(slab, h)],
            out_send.at[h, to], out_recv.at[h, slab], to * 4 + r, panel,
        )

    def others(visit):
        @pl.loop(1, 4)
        def _(i):
            visit((r + i) % 4)

    def own_level0(h):
        @pl.loop(0, 4)
        def _(i):
            f = (y + i + i // 2 - 2 * (i // 3)) % 4
            others(lambda owner: piv0_of(h, f, owner, r).wait_recv())
            upper[h, f] = jnp.dot(
                inv[f], piv0[h, pl.ds(f * 4, 4)].reshape(PANEL, HALF), preferred_element_type=F32
            ).astype(BF16)

            subtract(parent.at[h], pparent0, front.at[h], upper.at[h, f], f * 4, 32, 4)

        @pl.loop(0, 4)
        def _(f):
            others(lambda to: piv0_of(h, f, r, to).wait_send())

        @pl.loop(0, 8)
        def _(j):
            a = j + j // 4 * 4
            extend(front.at[h], parent.at[h], 1, a, a + 4)

        others(lambda to: piv1_of(h, r, to).start())

        @pl.loop(0, 16)
        def _(j):
            piv1[h, j, r] = parent[h, j, 0, 0:16, :]

    def own_level1(h):
        others(lambda owner: piv1_of(h, owner, r).wait_recv())

        @pl.loop(0, 2)
        def _(f):
            upper[h, f] = jnp.dot(
                inv[4 + f], piv1[h, pl.ds(f * 8, 8)].reshape(PANEL, HALF), preferred_element_type=F32
            ).astype(BF16)

            @pl.loop(0, 2)
            def _(j):
                subtract(parent.at[h], pparent1, front.at[h], upper.at[h, f], f * 8 + j * 4, 16, 4)

        others(lambda to: piv1_of(h, r, to).wait_send())

        @pl.loop(0, 8)
        def _(j):
            extend(front.at[h], parent.at[h], 2, j, j + 8)

        @pl.loop(0, 8)
        def _(j):
            pair = [parent[h, 2 * j + k, 0, 0:16, :].astype(F32)[0:8] for k in range(2)]
            piv2[h, r, j] = jnp.concatenate(pair, axis=0).astype(BF16)

        others(lambda to: piv2_of(h, r, to).start())

    def own_level2(h):
        others(lambda owner: piv2_of(h, owner, r).wait_recv())

        @pl.loop(0, 4)
        def _(owner):
            @pl.loop(0, 8)
            def _(j):
                both = piv2[h, owner, j].astype(F32)
                piv2_wide[2 * j, owner] = both[0:8]
                piv2_wide[2 * j + 1, owner] = both[8:16]

        upper[h, 0] = jnp.dot(
            inv[6], piv2_wide[...].reshape(PANEL, HALF).astype(BF16), preferred_element_type=F32
        ).astype(BF16)

        def finish(dy, dx):
            to = at(dy, dx)
            subtract(parent.at[h], pparent2, front.at[h], upper.at[h, 0], to, 8, 1)
            out_of(h, g, to).start()

        for stage in range(3):
            each_peer(stage, finish)
        subtract(parent.at[h], pparent2, front.at[h], upper.at[h, 0], g, 8, 1)
        home(h).start()

    def home(h):
        return pltpu.make_async_copy(front.at[h, g], out.at[:, :, columns(g, h)], local_sem.at[4 + h])

    for stage in range(3):
        open_stage(0, stage)
    spread_panel.pass_on()
    send_child(1, 0)
    spread_panel.take_direct()
    fwd_of(y, core).start()
    open_panel(y)
    others(lambda to: pp0_of(r, to).start())

    @pl.loop(0, 4)
    def _(j):
        ppiv0[j, r] = pparent0[y * 4 + j, 0, 0:32, piece]

    send_child(1, 1)
    inv_copy.wait()
    others(lambda owner: pp0_of(owner, r).wait_recv())
    half0 = pl.ds(multiple(core * 256, 256), 256)
    pupper0[y, half0, piece] = jnp.dot(
        inv[y, half0, :], ppiv0[...].reshape(PANEL, BLOCK), preferred_element_type=F32
    ).astype(BF16)
    spread_upper0.begin()

    @pl.loop(1, 4)
    def _(i):
        spread_panel.take_row(i)
        fwd_of((y + i) % 4, core).start()

    spread_upper0.pass_on()
    send_child(1, 2)

    @pl.loop(1, 4)
    def _(i):
        open_panel((y + i) % 4)

    own_level0(0)

    spread_upper0.take_direct()
    up0f_of(y, core).start()

    @pl.loop(1, 4)
    def _(i):
        spread_upper0.take_row(i)
        up0f_of((y + i) % 4, core).start()

    @pl.when(panel == 0)
    def _():
        for index in range(3):
            first_copy(0, 1, index).wait_send()

    spread_panel.sent()

    @pl.loop(0, 4)
    def _(f):
        fwd_of(f, core).wait_send()

    @pl.loop(0, 4)
    def _(i):
        f = (y + i) % 4
        up0f_of(f, 1 - core).wait_recv()

        subtract(pparent0, pparent0, pfront, pupper0.at[f], f * 4, 32, 4)

    @pl.loop(0, 8)
    def _(j):
        a = j + j // 4 * 4
        extend(pfront, pparent1, 1, a, a + 4)

    others(lambda to: pp1_of(r, to).start())

    @pl.loop(0, 8)
    def _(j):
        ppiv1[j, r] = pparent1[y // 2 * 8 + j, 0, 0:16, piece]

    open_stage(1, 0)
    open_stage(1, 1)
    own_level1(0)

    others(lambda owner: pp1_of(owner, r).wait_recv())
    quarter = pl.ds(multiple(core * 256 + y % 2 * BLOCK, BLOCK), BLOCK)
    pupper1[y // 2, quarter, piece] = jnp.dot(
        inv[4 + y // 2, quarter, :], ppiv1[...].reshape(PANEL, BLOCK), preferred_element_type=F32
    ).astype(BF16)
    spread_upper1.begin()
    open_stage(1, 2)
    spread_upper1.pass_on()
    own_level0(1)
    spread_upper1.take_direct()
    spread_upper1.take_passed()

    @pl.loop(0, 2)
    def _(f):
        up1f_of(f, core).start()

    @pl.loop(0, 2)
    def _(f):
        up1f_of(f, 1 - core).wait_recv()

        @pl.loop(0, 2)
        def _(j):
            subtract(pparent1, pparent1, pfront, pupper1.at[f], f * 8 + j * 4, 16, 4)

    @pl.loop(0, 8)
    def _(j):
        extend(pfront, pparent2, 2, j, j + 8)

    own_level2(0)
    own_level1(1)
    own_level2(1)

    for h in range(2):
        home(h).wait()

    def settle(dy, dx):
        slab = at(dy, dx)
        map_of(g, slab).wait_send()
        for h in range(2):
            out_of(h, slab, g).wait_recv()
            out_of(h, g, slab).wait_send()
            a2a_of(h, g, slab).wait_send()

    for stage in range(3):
        each_peer(stage, settle)
    spread_upper0.sent()
    spread_upper1.sent()

    @pl.loop(0, 4)
    def _(f):
        up0f_of(f, core).wait_send()

    @pl.loop(0, 2)
    def _(f):
        up1f_of(f, core).wait_send()

    def leave(to):
        pp0_of(r, to).wait_send()
        pp1_of(r, to).wait_send()
        for h in range(2):
            piv2_of(h, r, to).wait_send()

    others(leave)


def on_device(child_front, own_map, cross_map, pivot_inverse):
    rows, width = child_front.shape
    dma = pltpu.SemaphoreType.DMA
    call = pl.pallas_call(
        kernel,
        out_shape=jax.ShapeDtypeStruct((2, BLOCK, width), BF16),
        in_specs=[
            pl.BlockSpec(memory_space=pl.ANY),
            pl.BlockSpec(memory_space=pltpu.SMEM),
            pl.BlockSpec(memory_space=pltpu.SMEM),
            pl.BlockSpec(memory_space=pl.ANY),
        ],
        out_specs=pl.BlockSpec(memory_space=pl.ANY),
        scratch_shapes=[
            pltpu.VMEM((2, 16, 2, BLOCK, HALF), BF16),
            pltpu.VMEM((2, 16, 2, BLOCK, HALF), BF16),
            pltpu.VMEM((16, 2, BLOCK, PANEL), BF16),
            pltpu.VMEM((16, 2, BLOCK, PANEL), BF16),
            pltpu.VMEM((16, 2, BLOCK, PANEL), BF16),
            pltpu.VMEM((16, 2, BLOCK, PANEL), BF16),
            pltpu.VMEM((7, PANEL, PANEL), BF16),
            pltpu.VMEM((16, 8, 128), jnp.int32),
            pltpu.SMEM((16, 8, 128), jnp.int32),
            pltpu.VMEM((2, 16, 4, 32, HALF), BF16),
            pltpu.VMEM((2, 16, 4, 16, HALF), BF16),
            pltpu.VMEM((2, 4, 8, 16, HALF), BF16),
            pltpu.VMEM((16, 4, 8, HALF), F32),
            pltpu.VMEM((4, 4, 32, BLOCK), BF16),
            pltpu.VMEM((8, 4, 16, BLOCK), BF16),
            pltpu.VMEM((2, 4, PANEL, HALF), BF16),
            pltpu.VMEM((4, PANEL, PANEL), BF16),
            pltpu.VMEM((2, PANEL, PANEL), BF16),
            dma((16,)), dma((16,)), dma((2, 16)), dma((2, 16)), dma((3,)), dma((1,)),
            dma((4, 4)), dma((16,)), dma((4,)), dma((4,)), dma((2, 4, 4)), dma((2, 4, 4)),
            dma((2, 4)), dma((2, 4)), dma((2, 4)), dma((2, 4)), dma((4,)), dma((4,)),
            dma((4,)), dma((4,)), dma((4, 4)), dma((16,)), dma((4,)), dma((4,)),
            dma((4, 4)), dma((16,)), dma((2,)), dma((2,)), dma((2, 16)), dma((2, 16)), dma((6,)),
        ],
        compiler_params=pltpu.CompilerParams(
            collective_id=0, has_side_effects=True, vmem_limit_bytes=60 * 1024 * 1024
        ),
        cost_estimate=pl.CostEstimate(
            flops=9_000_000_000, bytes_accessed=16_000_000, transcendentals=0
        ),
    )
    tables = [table[:, 0, :].T for table in (own_map, cross_map)]
    result = call(child_front.reshape(2, BLOCK, width), *tables, pivot_inverse)
    return result.reshape(rows, width)


def solution(mesh):
    placed = (P("leaf", "panel"), P(None, "leaf", None), P(None, "leaf", None), P())
    return jax.shard_map(
        on_device, mesh=mesh, in_specs=placed, out_specs=P("leaf", "panel"), check_vma=False
    )
```

```python
import functools

import jax
import jax.numpy as jnp
from jax import lax
from jax.experimental import pallas as pl
from jax.experimental.pallas import tpu as pltpu
from jax.sharding import PartitionSpec as P

PANEL = 512
BLOCK = 128
WIDTH = 256
HALF = 128
MESH = pl.DeviceIdType.MESH
F32 = jnp.float32
BF16 = jnp.bfloat16


def multiple(value, of):
    return pl.multiple_of(value, of)


def kernel(
    child, own_map, cross_map, inverse, out,
    front_a, front_b, parent, pfront, pparent0, pparent1, pparent2, inv, map_buf, map_tab,
    piv0, piv1, piv2, piv2_wide, ppiv0, ppiv1, upper, pupper0, pupper1,
    map_send, map_recv, a2a_send, a2a_recv, first_send, first_recv,
    pan_send, pan_recv, fwd_send, fwd_recv, piv0_send, piv0_recv,
    piv1_send, piv1_recv, piv2_send, piv2_recv, pp0_send, pp0_recv,
    pp1_send, pp1_recv, up0_send, up0_recv, up0f_send, up0f_recv,
    up1_send, up1_recv, up1f_send, up1f_recv, out_send, out_recv, local_sem,
):
    fronts = (front_a, front_b)
    leaf = lax.axis_index("leaf")
    panel = lax.axis_index("panel")
    g, r = leaf // 4, leaf % 4
    y, x = g // 4, g % 4
    core = panel % 2
    mate = panel + 1 - 2 * core

    def at(dy, dx):
        return ((y + dy) % 4) * 4 + (x + dx) % 4

    def each_peer(stage, visit):
        if stage == 0:
            @pl.loop(1, 4)
            def _(i):
                visit(0, i)
        elif stage == 1:
            @pl.loop(0, 4)
            def _(i):
                visit(1, i)
                visit(3, i)
        else:
            @pl.loop(0, 4)
            def _(i):
                visit(2, i)

    def remote(src, dst, send, recv, to_leaf, to_panel):
        return pltpu.make_async_remote_copy(
            src_ref=src, dst_ref=dst, send_sem=send, recv_sem=recv,
            device_id=(to_leaf, to_panel), device_id_type=MESH,
        )

    def crossed(first, second):
        return at(core * first + (1 - core) * second, core * second + (1 - core) * first)

    class Spread:
        def __init__(self, part_of, send, recv):
            self.part_of, self.send, self.recv = part_of, send, recv

        def copy(self, slab, i, j, to):
            part = self.part_of(slab)
            return remote(part, part, self.send.at[i, j], self.recv.at[slab], to * 4 + r, panel)

        def begin(self):
            @pl.loop(1, 4)
            def _(i):
                self.copy(g, i, 0, crossed(i, 0)).start()
                self.copy(g, 0, i, crossed(0, i)).start()

        def pass_on(self):
            @pl.loop(1, 4)
            def _(i):
                slab = crossed(i, 0)
                self.copy(slab, 0, 0, g).wait_recv()

                @pl.loop(1, 4)
                def _(j):
                    self.copy(slab, i, j, crossed(0, j)).start()

        def take_direct(self):
            @pl.loop(1, 4)
            def _(j):
                self.copy(crossed(0, j), 0, 0, g).wait_recv()

        def take_row(self, dy):
            @pl.loop(1, 4)
            def _(i):
                self.copy(at(dy, i), 0, 0, g).wait_recv()

        def take_passed(self):
            @pl.loop(1, 4)
            def _(i):
                @pl.loop(1, 4)
                def _(j):
                    self.copy(crossed(i, j), 0, 0, g).wait_recv()

        def sent(self):
            @pl.loop(1, 4)
            def _(i):
                self.copy(g, i, 0, crossed(i, 0)).wait_send()
                self.copy(g, 0, i, crossed(0, i)).wait_send()

                @pl.loop(1, 4)
                def _(j):
                    self.copy(crossed(i, 0), i, j, crossed(0, j)).wait_send()

    barrier = pltpu.get_barrier_semaphore()

    def greet(dy, dx):
        pl.semaphore_signal(barrier, inc=1, device_id=(at(dy, dx) * 4 + r, panel), device_id_type=MESH)

    @pl.loop(1, 4)
    def _(i):
        pl.semaphore_signal(barrier, inc=1, device_id=(leaf, (panel + i) % 4), device_id_type=MESH)

    for stage in (2, 1, 0):
        each_peer(stage, greet)

    @pl.loop(1, 4)
    def _(i):
        pl.semaphore_signal(barrier, inc=1, device_id=(g * 4 + (r + i) % 4, panel), device_id_type=MESH)

    def columns(which, h):
        return pl.ds(multiple(which * WIDTH + h * HALF, HALF), HALF)

    def own_copy(h):
        return pltpu.make_async_copy(child.at[:, :, columns(g, h)], fronts[h].at[g], local_sem.at[4 + h])

    own_copy(0).start()
    own_copy(1).start()
    inv_copy = pltpu.make_async_copy(inverse, inv, local_sem.at[1])
    inv_copy.start()
    row = lax.broadcasted_iota(jnp.int32, (8, 128), 0)
    lane = lax.broadcasted_iota(jnp.int32, (8, 128), 1)
    table = jnp.zeros((8, 128), jnp.int32)
    for level in range(3):
        for slot in range(2):
            table = jnp.where((row == level) & (lane == slot), own_map[slot, level], table)
            table = jnp.where((row == level) & (lane == 2 + slot), cross_map[slot, level], table)
    map_buf[g] = table
    pl.semaphore_wait(barrier, 21)

    def first_copy(half, to_panel, index):
        return remote(
            child.at[half, :, pl.ds(0, PANEL)], pfront.at[g, half],
            first_send.at[index], first_recv.at[0], leaf, to_panel,
        )

    first_own = pltpu.make_async_copy(child.at[0, :, pl.ds(0, PANEL)], pfront.at[g, 0], local_sem.at[3])

    @pl.when(panel == 0)
    def _():
        first_copy(0, 2, 1).start()
        first_copy(1, 3, 2).start()
        first_copy(1, 1, 0).start()
        first_own.start()

    def map_of(slab, to):
        return remote(map_buf.at[slab], map_buf.at[slab], map_send.at[to], map_recv.at[slab], to * 4 + r, panel)

    def a2a_of(h, slab, to):
        return remote(
            child.at[:, :, columns(to, h)], fronts[h].at[slab],
            a2a_send.at[h, to], a2a_recv.at[h, slab], to * 4 + r, panel,
        )

    spread_panel = Spread(lambda slab: pfront.at[slab, core], pan_send, pan_recv)

    def send_child(h, stage):
        each_peer(stage, lambda dy, dx: a2a_of(h, g, at(dy, dx)).start())

    for stage in range(3):
        each_peer(stage, lambda dy, dx: map_of(g, at(dy, dx)).start())
    for stage in range(3):
        send_child(0, stage)

    @pl.when(panel == 0)
    def _():
        first_own.wait()

    @pl.when(panel != 0)
    def _():
        first_copy(core, panel, 0).wait_recv()

    spread_panel.begin()


    def take_map(dy, dx):
        map_of(at(dy, dx), g).wait_recv()

    for stage in range(3):
        each_peer(stage, take_map)
    to_smem = pltpu.make_async_copy(map_buf, map_tab, local_sem.at[2])
    to_smem.start()
    to_smem.wait()

    def extend(src, dst, level, a, b):
        width = src.shape[3]
        step = min(width, WIDTH)
        for mine, other in ((a, b), (b, a)):
            for slot in range(2):
                own_block = map_tab[mine, level, slot]
                cross_block = map_tab[mine, level, 2 + slot]

                @pl.loop(0, BLOCK // 32)
                def _(q):
                    for left in range(0, width, step):
                        part = (pl.ds(multiple(q * 32, 32), 32), pl.ds(left, step))
                        if level:
                            kept, moved = src[(mine, own_block) + part], src[(other, cross_block) + part]
                        else:
                            kept = jnp.where(own_block == 0, src[(mine, 0) + part], src[(mine, 1) + part])
                            moved = jnp.where(cross_block == 0, src[(other, 0) + part], src[(other, 1) + part])
                        dst[(mine, slot) + part] = (kept.astype(F32) + moved.astype(F32)).astype(BF16)

    def subtract(src, columns_of, dst, factor, slab, rows, count=2):
        width = src.shape[3]
        step = min(width, WIDTH)
        slabs = pl.ds(slab, count)
        left = columns_of[slabs].reshape(count * 2 * BLOCK, PANEL)
        for low in range(0, width, step):
            part = pl.ds(low, step)
            product = jnp.dot(left, factor[:, part], preferred_element_type=F32)
            start = src[slabs, :, :, part].reshape(count * 2 * BLOCK, step).astype(F32)
            dst[slabs, :, :, part] = (start - product).astype(BF16).reshape(count, 2, BLOCK, step)
        for k in range(count):
            if rows % 16:
                keep = lax.broadcasted_iota(jnp.int32, (16, width), 0) >= rows
                top = dst[slab + k, 0, 0:16, :].astype(F32)
                dst[slab + k, 0, 0:16, :] = jnp.where(keep, top, 0.0).astype(BF16)
            else:
                dst[slab + k, 0, 0:rows, :] = jnp.zeros((rows, width), BF16)

    def piv0_of(h, f, owner, to):
        slabs = pl.ds(f * 4, 4)
        return remote(
            parent.at[h, slabs, 0, pl.ds(0, 32), :], piv0.at[h, slabs, owner],
            piv0_send.at[h, f, to], piv0_recv.at[h, f, owner], g * 4 + to, panel,
        )

    def fwd_of(f, half):
        part = pfront.at[pl.ds(f * 4, 4), half]
        return remote(part, part, fwd_send.at[f], fwd_recv.at[f], leaf, mate)

    def open_front(h, f):
        @pl.loop(0, 2)
        def _(j):
            extend(fronts[h], parent.at[h], 0, f * 4 + j, f * 4 + j + 2)

        @pl.loop(1, 4)
        def _(i):
            piv0_of(h, f, r, (r + i) % 4).start()

        @pl.loop(0, 4)
        def _(j):
            piv0[h, f * 4 + j, r] = parent[h, f * 4 + j, 0, 0:32, :]

    def open_stage(h, stage):
        each_peer(stage, lambda dy, dx: a2a_of(h, at(dy, dx), g).wait_recv())
        if stage == 0:
            own_copy(h).wait()
            open_front(h, y)
        elif stage == 1:
            @pl.loop(0, 2)
            def _(i):
                open_front(h, (y + 1 + 2 * i) % 4)
        else:
            open_front(h, (y + 2) % 4)

    def open_panel(f):
        fwd_of(f, 1 - core).wait_recv()

        @pl.loop(0, 2)
        def _(j):
            extend(pfront, pparent0, 0, f * 4 + j, f * 4 + j + 2)

    piece = pl.ds(multiple(x * BLOCK, BLOCK), BLOCK)

    def pp0_of(owner, to):
        return remote(
            pparent0.at[pl.ds(y * 4, 4), 0, pl.ds(0, 32), piece], ppiv0.at[:, owner],
            pp0_send.at[to], pp0_recv.at[owner], g * 4 + to, panel,
        )

    spread_upper0 = Spread(
        lambda slab: pupper0.at[
            slab // 4, pl.ds(multiple(core * 256, 256), 256), pl.ds(multiple(slab % 4 * BLOCK, BLOCK), BLOCK)
        ],
        up0_send, up0_recv,
    )

    def up0f_of(f, half):
        part = pupper0.at[f, pl.ds(multiple(half * 256, 256), 256), :]
        return remote(part, part, up0f_send.at[f], up0f_recv.at[f], leaf, mate)

    def piv1_of(h, owner, to):
        return remote(
            parent.at[h, :, 0, pl.ds(0, 16), :], piv1.at[h, :, owner],
            piv1_send.at[h, to], piv1_recv.at[h, owner], g * 4 + to, panel,
        )

    def pp1_of(owner, to):
        return remote(
            pparent1.at[pl.ds(y // 2 * 8, 8), 0, pl.ds(0, 16), piece], ppiv1.at[:, owner],
            pp1_send.at[to], pp1_recv.at[owner], g * 4 + to, panel,
        )

    spread_upper1 = Spread(
        lambda slab: pupper1.at[
            slab // 8,
            pl.ds(multiple(core * 256 + slab // 4 % 2 * BLOCK, BLOCK), BLOCK),
            pl.ds(multiple(slab % 4 * BLOCK, BLOCK), BLOCK),
        ],
        up1_send, up1_recv,
    )

    def up1f_of(f, half):
        part = pupper1.at[f, pl.ds(multiple(half * 256, 256), 256), :]
        return remote(part, part, up1f_send.at[f], up1f_recv.at[f], leaf, mate)

    def piv2_of(h, owner, to):
        part = piv2.at[h, owner]
        return remote(part, part, piv2_send.at[h, to], piv2_recv.at[h, owner], g * 4 + to, panel)

    def out_of(h, slab, to):
        return remote(
            fronts[h].at[to], out.at[:, :, columns(slab, h)],
            out_send.at[h, to], out_recv.at[h, slab], to * 4 + r, panel,
        )

    def others(visit):
        @pl.loop(1, 4)
        def _(i):
            visit((r + i) % 4)

    def own_level0(h):
        @pl.loop(0, 4)
        def _(i):
            f = (y + i + i // 2 - 2 * (i // 3)) % 4
            others(lambda owner: piv0_of(h, f, owner, r).wait_recv())
            upper[h, f] = jnp.dot(
                inv[f], piv0[h, pl.ds(f * 4, 4)].reshape(PANEL, HALF), preferred_element_type=F32
            ).astype(BF16)

            subtract(parent.at[h], pparent0, fronts[h], upper.at[h, f], f * 4, 32, 4)

        @pl.loop(0, 4)
        def _(f):
            others(lambda to: piv0_of(h, f, r, to).wait_send())

        @pl.loop(0, 8)
        def _(j):
            a = j + j // 4 * 4
            extend(fronts[h], parent.at[h], 1, a, a + 4)

        others(lambda to: piv1_of(h, r, to).start())

        @pl.loop(0, 16)
        def _(j):
            piv1[h, j, r] = parent[h, j, 0, 0:16, :]

    def own_level1(h):
        others(lambda owner: piv1_of(h, owner, r).wait_recv())

        @pl.loop(0, 2)
        def _(f):
            upper[h, f] = jnp.dot(
                inv[4 + f], piv1[h, pl.ds(f * 8, 8)].reshape(PANEL, HALF), preferred_element_type=F32
            ).astype(BF16)

            @pl.loop(0, 2)
            def _(j):
                subtract(parent.at[h], pparent1, fronts[h], upper.at[h, f], f * 8 + j * 4, 16, 4)

        others(lambda to: piv1_of(h, r, to).wait_send())

        @pl.loop(0, 8)
        def _(j):
            extend(fronts[h], parent.at[h], 2, j, j + 8)

        @pl.loop(0, 8)
        def _(j):
            pair = [parent[h, 2 * j + k, 0, 0:16, :].astype(F32)[0:8] for k in range(2)]
            piv2[h, r, j] = jnp.concatenate(pair, axis=0).astype(BF16)

        others(lambda to: piv2_of(h, r, to).start())

    def own_level2(h):
        others(lambda owner: piv2_of(h, owner, r).wait_recv())

        @pl.loop(0, 4)
        def _(owner):
            @pl.loop(0, 8)
            def _(j):
                both = piv2[h, owner, j].astype(F32)
                piv2_wide[2 * j, owner] = both[0:8]
                piv2_wide[2 * j + 1, owner] = both[8:16]

        upper[h, 0] = jnp.dot(
            inv[6], piv2_wide[...].reshape(PANEL, HALF).astype(BF16), preferred_element_type=F32
        ).astype(BF16)

        def finish(dy, dx):
            to = at(dy, dx)
            subtract(parent.at[h], pparent2, fronts[h], upper.at[h, 0], to, 8, 1)
            out_of(h, g, to).start()

        for stage in range(3):
            each_peer(stage, finish)
        subtract(parent.at[h], pparent2, fronts[h], upper.at[h, 0], g, 8, 1)
        home(h).start()

    def home(h):
        return pltpu.make_async_copy(fronts[h].at[g], out.at[:, :, columns(g, h)], local_sem.at[4 + h])

    for stage in range(3):
        open_stage(0, stage)
    spread_panel.pass_on()
    send_child(1, 0)
    spread_panel.take_direct()
    fwd_of(y, core).start()
    open_panel(y)
    others(lambda to: pp0_of(r, to).start())

    @pl.loop(0, 4)
    def _(j):
        ppiv0[j, r] = pparent0[y * 4 + j, 0, 0:32, piece]

    send_child(1, 1)
    inv_copy.wait()
    others(lambda owner: pp0_of(owner, r).wait_recv())
    half0 = pl.ds(multiple(core * 256, 256), 256)
    pupper0[y, half0, piece] = jnp.dot(
        inv[y, half0, :], ppiv0[...].reshape(PANEL, BLOCK), preferred_element_type=F32
    ).astype(BF16)
    spread_upper0.begin()

    @pl.loop(1, 4)
    def _(i):
        spread_panel.take_row(i)
        fwd_of((y + i) % 4, core).start()

    spread_upper0.pass_on()
    send_child(1, 2)

    @pl.loop(1, 4)
    def _(i):
        open_panel((y + i) % 4)

    own_level0(0)

    spread_upper0.take_direct()
    up0f_of(y, core).start()

    @pl.loop(1, 4)
    def _(i):
        spread_upper0.take_row(i)
        up0f_of((y + i) % 4, core).start()

    @pl.when(panel == 0)
    def _():
        for index in range(3):
            first_copy(0, 1, index).wait_send()

    spread_panel.sent()

    @pl.loop(0, 4)
    def _(f):
        fwd_of(f, core).wait_send()

    @pl.loop(0, 4)
    def _(i):
        f = (y + i) % 4
        up0f_of(f, 1 - core).wait_recv()

        subtract(pparent0, pparent0, pfront, pupper0.at[f], f * 4, 32, 4)

    @pl.loop(0, 8)
    def _(j):
        a = j + j // 4 * 4
        extend(pfront, pparent1, 1, a, a + 4)

    others(lambda to: pp1_of(r, to).start())

    @pl.loop(0, 8)
    def _(j):
        ppiv1[j, r] = pparent1[y // 2 * 8 + j, 0, 0:16, piece]

    open_stage(1, 0)
    open_stage(1, 1)
    open_stage(1, 2)
    own_level1(0)

    others(lambda owner: pp1_of(owner, r).wait_recv())
    quarter = pl.ds(multiple(core * 256 + y % 2 * BLOCK, BLOCK), BLOCK)
    pupper1[y // 2, quarter, piece] = jnp.dot(
        inv[4 + y // 2, quarter, :], ppiv1[...].reshape(PANEL, BLOCK), preferred_element_type=F32
    ).astype(BF16)
    spread_upper1.begin()
    spread_upper1.pass_on()
    own_level0(1)
    spread_upper1.take_direct()
    spread_upper1.take_passed()

    @pl.loop(0, 2)
    def _(f):
        up1f_of(f, core).start()

    @pl.loop(0, 2)
    def _(f):
        up1f_of(f, 1 - core).wait_recv()

        @pl.loop(0, 2)
        def _(j):
            subtract(pparent1, pparent1, pfront, pupper1.at[f], f * 8 + j * 4, 16, 4)

    @pl.loop(0, 8)
    def _(j):
        extend(pfront, pparent2, 2, j, j + 8)

    own_level2(0)
    own_level1(1)
    own_level2(1)

    for h in range(2):
        home(h).wait()

    def settle(dy, dx):
        slab = at(dy, dx)
        map_of(g, slab).wait_send()
        for h in range(2):
            out_of(h, slab, g).wait_recv()
            out_of(h, g, slab).wait_send()
            a2a_of(h, g, slab).wait_send()

    for stage in range(3):
        each_peer(stage, settle)
    spread_upper0.sent()
    spread_upper1.sent()

    @pl.loop(0, 4)
    def _(f):
        up0f_of(f, core).wait_send()

    @pl.loop(0, 2)
    def _(f):
        up1f_of(f, core).wait_send()

    def leave(to):
        pp0_of(r, to).wait_send()
        pp1_of(r, to).wait_send()
        for h in range(2):
            piv2_of(h, r, to).wait_send()

    others(leave)


def on_device(child_front, own_map, cross_map, pivot_inverse):
    rows, width = child_front.shape
    dma = pltpu.SemaphoreType.DMA
    call = pl.pallas_call(
        kernel,
        out_shape=jax.ShapeDtypeStruct((2, BLOCK, width), BF16),
        in_specs=[
            pl.BlockSpec(memory_space=pl.ANY),
            pl.BlockSpec(memory_space=pltpu.SMEM),
            pl.BlockSpec(memory_space=pltpu.SMEM),
            pl.BlockSpec(memory_space=pl.ANY),
        ],
        out_specs=pl.BlockSpec(memory_space=pl.ANY),
        scratch_shapes=[
            pltpu.VMEM((16, 2, BLOCK, HALF), BF16),
            pltpu.VMEM((16, 2, BLOCK, HALF), BF16),
            pltpu.VMEM((2, 16, 2, BLOCK, HALF), BF16),
            pltpu.VMEM((16, 2, BLOCK, PANEL), BF16),
            pltpu.VMEM((16, 2, BLOCK, PANEL), BF16),
            pltpu.VMEM((16, 2, BLOCK, PANEL), BF16),
            pltpu.VMEM((16, 2, BLOCK, PANEL), BF16),
            pltpu.VMEM((7, PANEL, PANEL), BF16),
            pltpu.VMEM((16, 8, 128), jnp.int32),
            pltpu.SMEM((16, 8, 128), jnp.int32),
            pltpu.VMEM((2, 16, 4, 32, HALF), BF16),
            pltpu.VMEM((2, 16, 4, 16, HALF), BF16),
            pltpu.VMEM((2, 4, 8, 16, HALF), BF16),
            pltpu.VMEM((16, 4, 8, HALF), F32),
            pltpu.VMEM((4, 4, 32, BLOCK), BF16),
            pltpu.VMEM((8, 4, 16, BLOCK), BF16),
            pltpu.VMEM((2, 4, PANEL, HALF), BF16),
            pltpu.VMEM((4, PANEL, PANEL), BF16),
            pltpu.VMEM((2, PANEL, PANEL), BF16),
            dma((16,)), dma((16,)), dma((2, 16)), dma((2, 16)), dma((3,)), dma((1,)),
            dma((4, 4)), dma((16,)), dma((4,)), dma((4,)), dma((2, 4, 4)), dma((2, 4, 4)),
            dma((2, 4)), dma((2, 4)), dma((2, 4)), dma((2, 4)), dma((4,)), dma((4,)),
            dma((4,)), dma((4,)), dma((4, 4)), dma((16,)), dma((4,)), dma((4,)),
            dma((4, 4)), dma((16,)), dma((2,)), dma((2,)), dma((2, 16)), dma((2, 16)), dma((6,)),
        ],
        compiler_params=pltpu.CompilerParams(
            collective_id=0, has_side_effects=True, vmem_limit_bytes=60 * 1024 * 1024
        ),
        cost_estimate=pl.CostEstimate(
            flops=9_000_000_000, bytes_accessed=16_000_000, transcendentals=0
        ),
    )
    tables = [table[:, 0, :].T for table in (own_map, cross_map)]
    result = call(child_front.reshape(2, BLOCK, width), *tables, pivot_inverse)
    return result.reshape(rows, width)


def solution(mesh):
    placed = (P("leaf", "panel"), P(None, "leaf", None), P(None, "leaf", None), P())
    return jax.shard_map(
        on_device, mesh=mesh, in_specs=placed, out_specs=P("leaf", "panel"), check_vma=False
    )
```

```python
import functools

import jax
import jax.numpy as jnp
from jax import lax
from jax.experimental import pallas as pl
from jax.experimental.pallas import tpu as pltpu
from jax.sharding import PartitionSpec as P

PANEL = 512
BLOCK = 128
WIDTH = 256
HALF = 128
MESH = pl.DeviceIdType.MESH
F32 = jnp.float32
BF16 = jnp.bfloat16


def multiple(value, of):
    return pl.multiple_of(value, of)


def kernel(
    child, own_map, cross_map, inverse, out,
    front_a, front_b, parent, pfront, pparent0, pparent1, pparent2, inv, map_buf, map_tab,
    piv0, piv1, piv2, piv2_wide, ppiv0, ppiv1, upper, pupper0, pupper1,
    map_send, map_recv, a2a_send, a2a_recv, first_send, first_recv,
    pan_send, pan_recv, fwd_send, fwd_recv, piv0_send, piv0_recv,
    piv1_send, piv1_recv, piv2_send, piv2_recv, pp0_send, pp0_recv,
    pp1_send, pp1_recv, up0_send, up0_recv, up0f_send, up0f_recv,
    up1_send, up1_recv, up1f_send, up1f_recv, out_send, out_recv, local_sem,
):
    fronts = (front_a, front_b)
    leaf = lax.axis_index("leaf")
    panel = lax.axis_index("panel")
    g, r = leaf // 4, leaf % 4
    y, x = g // 4, g % 4
    core = panel % 2
    mate = panel + 1 - 2 * core

    def at(dy, dx):
        return ((y + dy) % 4) * 4 + (x + dx) % 4

    def each_peer(stage, visit):
        if stage == 0:
            @pl.loop(1, 4)
            def _(i):
                visit(0, i)
        elif stage == 1:
            @pl.loop(0, 4)
            def _(i):
                visit(1, i)
                visit(3, i)
        else:
            @pl.loop(0, 4)
            def _(i):
                visit(2, i)

    def remote(src, dst, send, recv, to_leaf, to_panel):
        return pltpu.make_async_remote_copy(
            src_ref=src, dst_ref=dst, send_sem=send, recv_sem=recv,
            device_id=(to_leaf, to_panel), device_id_type=MESH,
        )

    def crossed(first, second):
        return at(core * first + (1 - core) * second, core * second + (1 - core) * first)

    class Spread:
        def __init__(self, part_of, send, recv):
            self.part_of, self.send, self.recv = part_of, send, recv

        def copy(self, slab, i, j, to):
            part = self.part_of(slab)
            return remote(part, part, self.send.at[i, j], self.recv.at[slab], to * 4 + r, panel)

        def begin(self):
            @pl.loop(1, 4)
            def _(i):
                self.copy(g, i, 0, crossed(i, 0)).start()
                self.copy(g, 0, i, crossed(0, i)).start()

        def pass_on(self):
            @pl.loop(1, 4)
            def _(i):
                slab = crossed(i, 0)
                self.copy(slab, 0, 0, g).wait_recv()

                @pl.loop(1, 4)
                def _(j):
                    self.copy(slab, i, j, crossed(0, j)).start()

        def take_direct(self):
            @pl.loop(1, 4)
            def _(j):
                self.copy(crossed(0, j), 0, 0, g).wait_recv()

        def take_row(self, dy):
            @pl.loop(1, 4)
            def _(i):
                self.copy(at(dy, i), 0, 0, g).wait_recv()

        def take_passed(self):
            @pl.loop(1, 4)
            def _(i):
                @pl.loop(1, 4)
                def _(j):
                    self.copy(crossed(i, j), 0, 0, g).wait_recv()

        def sent(self):
            @pl.loop(1, 4)
            def _(i):
                self.copy(g, i, 0, crossed(i, 0)).wait_send()
                self.copy(g, 0, i, crossed(0, i)).wait_send()

                @pl.loop(1, 4)
                def _(j):
                    self.copy(crossed(i, 0), i, j, crossed(0, j)).wait_send()

    barrier = pltpu.get_barrier_semaphore()

    def greet(dy, dx):
        pl.semaphore_signal(barrier, inc=1, device_id=(at(dy, dx) * 4 + r, panel), device_id_type=MESH)

    @pl.loop(1, 4)
    def _(i):
        pl.semaphore_signal(barrier, inc=1, device_id=(leaf, (panel + i) % 4), device_id_type=MESH)

    for stage in (2, 1, 0):
        each_peer(stage, greet)

    @pl.loop(1, 4)
    def _(i):
        pl.semaphore_signal(barrier, inc=1, device_id=(g * 4 + (r + i) % 4, panel), device_id_type=MESH)

    def columns(which, h):
        return pl.ds(multiple(which * WIDTH + h * HALF, HALF), HALF)

    def own_copy(h):
        return pltpu.make_async_copy(child.at[:, :, columns(g, h)], fronts[h].at[g], local_sem.at[4 + h])

    own_copy(0).start()
    own_copy(1).start()
    inv_copy = pltpu.make_async_copy(inverse, inv, local_sem.at[1])
    inv_copy.start()
    row = lax.broadcasted_iota(jnp.int32, (8, 128), 0)
    lane = lax.broadcasted_iota(jnp.int32, (8, 128), 1)
    table = jnp.zeros((8, 128), jnp.int32)
    for level in range(3):
        for slot in range(2):
            table = jnp.where((row == level) & (lane == slot), own_map[slot, level], table)
            table = jnp.where((row == level) & (lane == 2 + slot), cross_map[slot, level], table)
    map_buf[g] = table
    pl.semaphore_wait(barrier, 21)

    def first_copy(half, to_panel, index):
        return remote(
            child.at[half, :, pl.ds(0, PANEL)], pfront.at[g, half],
            first_send.at[index], first_recv.at[0], leaf, to_panel,
        )

    first_own = pltpu.make_async_copy(child.at[0, :, pl.ds(0, PANEL)], pfront.at[g, 0], local_sem.at[3])

    @pl.when(panel == 0)
    def _():
        first_copy(0, 2, 1).start()
        first_copy(1, 3, 2).start()
        first_copy(1, 1, 0).start()
        first_own.start()

    def map_of(slab, to):
        return remote(map_buf.at[slab], map_buf.at[slab], map_send.at[to], map_recv.at[slab], to * 4 + r, panel)

    def a2a_of(h, slab, to):
        return remote(
            child.at[:, :, columns(to, h)], fronts[h].at[slab],
            a2a_send.at[h, to], a2a_recv.at[h, slab], to * 4 + r, panel,
        )

    spread_panel = Spread(lambda slab: pfront.at[slab, core], pan_send, pan_recv)

    def send_child(h, stage):
        each_peer(stage, lambda dy, dx: a2a_of(h, g, at(dy, dx)).start())

    for stage in range(3):
        each_peer(stage, lambda dy, dx: map_of(g, at(dy, dx)).start())
    for stage in range(3):
        send_child(0, stage)

    @pl.when(panel == 0)
    def _():
        first_own.wait()

    @pl.when(panel != 0)
    def _():
        first_copy(core, panel, 0).wait_recv()

    spread_panel.begin()


    def take_map(dy, dx):
        map_of(at(dy, dx), g).wait_recv()

    for stage in range(3):
        each_peer(stage, take_map)
    to_smem = pltpu.make_async_copy(map_buf, map_tab, local_sem.at[2])
    to_smem.start()
    to_smem.wait()

    def extend(src, dst, level, a, b):
        width = src.shape[3]
        step = min(width, WIDTH)
        for mine, other in ((a, b), (b, a)):
            for slot in range(2):
                own_block = map_tab[mine, level, slot]
                cross_block = map_tab[mine, level, 2 + slot]

                @pl.loop(0, BLOCK // 32)
                def _(q):
                    for left in range(0, width, step):
                        part = (pl.ds(multiple(q * 32, 32), 32), pl.ds(left, step))
                        if level:
                            kept, moved = src[(mine, own_block) + part], src[(other, cross_block) + part]
                        else:
                            kept = jnp.where(own_block == 0, src[(mine, 0) + part], src[(mine, 1) + part])
                            moved = jnp.where(cross_block == 0, src[(other, 0) + part], src[(other, 1) + part])
                        dst[(mine, slot) + part] = (kept.astype(F32) + moved.astype(F32)).astype(BF16)

    def subtract(src, columns_of, dst, factor, slab, rows, count=2):
        width = src.shape[3]
        step = min(width, WIDTH)
        slabs = pl.ds(slab, count)
        left = columns_of[slabs].reshape(count * 2 * BLOCK, PANEL)
        for low in range(0, width, step):
            part = pl.ds(low, step)
            product = jnp.dot(left, factor[:, part], preferred_element_type=F32)
            start = src[slabs, :, :, part].reshape(count * 2 * BLOCK, step).astype(F32)
            dst[slabs, :, :, part] = (start - product).astype(BF16).reshape(count, 2, BLOCK, step)
        for k in range(count):
            if rows % 16:
                keep = lax.broadcasted_iota(jnp.int32, (16, width), 0) >= rows
                top = dst[slab + k, 0, 0:16, :].astype(F32)
                dst[slab + k, 0, 0:16, :] = jnp.where(keep, top, 0.0).astype(BF16)
            else:
                dst[slab + k, 0, 0:rows, :] = jnp.zeros((rows, width), BF16)

    def piv0_of(h, f, owner, to):
        slabs = pl.ds(f * 4, 4)
        return remote(
            parent.at[h, slabs, 0, pl.ds(0, 32), :], piv0.at[h, slabs, owner],
            piv0_send.at[h, f, to], piv0_recv.at[h, f, owner], g * 4 + to, panel,
        )

    def fwd_of(f, half):
        part = pfront.at[pl.ds(f * 4, 4), half]
        return remote(part, part, fwd_send.at[f], fwd_recv.at[f], leaf, mate)

    def open_front(h, f):
        @pl.loop(0, 2)
        def _(j):
            extend(fronts[h], parent.at[h], 0, f * 4 + j, f * 4 + j + 2)

        @pl.loop(1, 4)
        def _(i):
            piv0_of(h, f, r, (r + i) % 4).start()

        @pl.loop(0, 4)
        def _(j):
            piv0[h, f * 4 + j, r] = parent[h, f * 4 + j, 0, 0:32, :]

    def open_stage(h, stage):
        each_peer(stage, lambda dy, dx: a2a_of(h, at(dy, dx), g).wait_recv())
        if stage == 0:
            own_copy(h).wait()
            open_front(h, y)
        elif stage == 1:
            @pl.loop(0, 2)
            def _(i):
                open_front(h, (y + 1 + 2 * i) % 4)
        else:
            open_front(h, (y + 2) % 4)

    def open_panel(f):
        fwd_of(f, 1 - core).wait_recv()

        @pl.loop(0, 2)
        def _(j):
            extend(pfront, pparent0, 0, f * 4 + j, f * 4 + j + 2)

    piece = pl.ds(multiple(x * BLOCK, BLOCK), BLOCK)

    def pp0_of(owner, to):
        return remote(
            pparent0.at[pl.ds(y * 4, 4), 0, pl.ds(0, 32), piece], ppiv0.at[:, owner],
            pp0_send.at[to], pp0_recv.at[owner], g * 4 + to, panel,
        )

    spread_upper0 = Spread(
        lambda slab: pupper0.at[
            slab // 4, pl.ds(multiple(core * 256, 256), 256), pl.ds(multiple(slab % 4 * BLOCK, BLOCK), BLOCK)
        ],
        up0_send, up0_recv,
    )

    def up0f_of(f, half):
        part = pupper0.at[f, pl.ds(multiple(half * 256, 256), 256), :]
        return remote(part, part, up0f_send.at[f], up0f_recv.at[f], leaf, mate)

    def piv1_of(h, owner, to):
        return remote(
            parent.at[h, :, 0, pl.ds(0, 16), :], piv1.at[h, :, owner],
            piv1_send.at[h, to], piv1_recv.at[h, owner], g * 4 + to, panel,
        )

    def pp1_of(owner, to):
        return remote(
            pparent1.at[pl.ds(y // 2 * 8, 8), 0, pl.ds(0, 16), piece], ppiv1.at[:, owner],
            pp1_send.at[to], pp1_recv.at[owner], g * 4 + to, panel,
        )

    spread_upper1 = Spread(
        lambda slab: pupper1.at[
            slab // 8,
            pl.ds(multiple(core * 256 + slab // 4 % 2 * BLOCK, BLOCK), BLOCK),
            pl.ds(multiple(slab % 4 * BLOCK, BLOCK), BLOCK),
        ],
        up1_send, up1_recv,
    )

    def up1f_of(f, half):
        part = pupper1.at[f, pl.ds(multiple(half * 256, 256), 256), :]
        return remote(part, part, up1f_send.at[f], up1f_recv.at[f], leaf, mate)

    def piv2_of(h, owner, to):
        part = piv2.at[h, owner]
        return remote(part, part, piv2_send.at[h, to], piv2_recv.at[h, owner], g * 4 + to, panel)

    def out_of(h, slab, to):
        return remote(
            fronts[h].at[to], out.at[:, :, columns(slab, h)],
            out_send.at[h, to], out_recv.at[h, slab], to * 4 + r, panel,
        )

    def others(visit):
        @pl.loop(1, 4)
        def _(i):
            visit((r + i) % 4)

    def own_level0(h):
        @pl.loop(0, 4)
        def _(i):
            f = (y + i + i // 2 - 2 * (i // 3)) % 4
            others(lambda owner: piv0_of(h, f, owner, r).wait_recv())
            upper[h, f] = jnp.dot(
                inv[f], piv0[h, pl.ds(f * 4, 4)].reshape(PANEL, HALF), preferred_element_type=F32
            ).astype(BF16)

            subtract(parent.at[h], pparent0, fronts[h], upper.at[h, f], f * 4, 32, 4)

        @pl.loop(0, 4)
        def _(f):
            others(lambda to: piv0_of(h, f, r, to).wait_send())

        @pl.loop(0, 8)
        def _(j):
            a = j + j // 4 * 4
            extend(fronts[h], parent.at[h], 1, a, a + 4)

        others(lambda to: piv1_of(h, r, to).start())

        @pl.loop(0, 16)
        def _(j):
            piv1[h, j, r] = parent[h, j, 0, 0:16, :]

    def own_level1(h):
        others(lambda owner: piv1_of(h, owner, r).wait_recv())

        @pl.loop(0, 2)
        def _(f):
            upper[h, f] = jnp.dot(
                inv[4 + f], piv1[h, pl.ds(f * 8, 8)].reshape(PANEL, HALF), preferred_element_type=F32
            ).astype(BF16)

            @pl.loop(0, 2)
            def _(j):
                subtract(parent.at[h], pparent1, fronts[h], upper.at[h, f], f * 8 + j * 4, 16, 4)

        others(lambda to: piv1_of(h, r, to).wait_send())

        @pl.loop(0, 8)
        def _(j):
            extend(fronts[h], parent.at[h], 2, j, j + 8)

        @pl.loop(0, 8)
        def _(j):
            pair = [parent[h, 2 * j + k, 0, 0:16, :].astype(F32)[0:8] for k in range(2)]
            piv2[h, r, j] = jnp.concatenate(pair, axis=0).astype(BF16)

        others(lambda to: piv2_of(h, r, to).start())

    def own_level2(h):
        others(lambda owner: piv2_of(h, owner, r).wait_recv())

        @pl.loop(0, 4)
        def _(owner):
            @pl.loop(0, 8)
            def _(j):
                both = piv2[h, owner, j].astype(F32)
                piv2_wide[2 * j, owner] = both[0:8]
                piv2_wide[2 * j + 1, owner] = both[8:16]

        upper[h, 0] = jnp.dot(
            inv[6], piv2_wide[...].reshape(PANEL, HALF).astype(BF16), preferred_element_type=F32
        ).astype(BF16)

        def finish(dy, dx):
            to = at(dy, dx)
            subtract(parent.at[h], pparent2, fronts[h], upper.at[h, 0], to, 8, 1)
            out_of(h, g, to).start()

        for stage in range(3):
            each_peer(stage, finish)
        subtract(parent.at[h], pparent2, fronts[h], upper.at[h, 0], g, 8, 1)
        home(h).start()

    def home(h):
        return pltpu.make_async_copy(fronts[h].at[g], out.at[:, :, columns(g, h)], local_sem.at[4 + h])

    for stage in range(3):
        open_stage(0, stage)
    spread_panel.pass_on()
    send_child(1, 0)
    spread_panel.take_direct()
    fwd_of(y, core).start()
    open_panel(y)
    others(lambda to: pp0_of(r, to).start())

    @pl.loop(0, 4)
    def _(j):
        ppiv0[j, r] = pparent0[y * 4 + j, 0, 0:32, piece]

    send_child(1, 1)
    inv_copy.wait()
    others(lambda owner: pp0_of(owner, r).wait_recv())
    half0 = pl.ds(multiple(core * 256, 256), 256)
    pupper0[y, half0, piece] = jnp.dot(
        inv[y, half0, :], ppiv0[...].reshape(PANEL, BLOCK), preferred_element_type=F32
    ).astype(BF16)
    spread_upper0.begin()

    @pl.loop(1, 4)
    def _(i):
        spread_panel.take_row(i)
        fwd_of((y + i) % 4, core).start()

    spread_upper0.pass_on()
    send_child(1, 2)

    @pl.loop(1, 4)
    def _(i):
        open_panel((y + i) % 4)

    own_level0(0)

    spread_upper0.take_direct()
    up0f_of(y, core).start()

    @pl.loop(1, 4)
    def _(i):
        spread_upper0.take_row(i)
        up0f_of((y + i) % 4, core).start()

    @pl.when(panel == 0)
    def _():
        for index in range(3):
            first_copy(0, 1, index).wait_send()

    spread_panel.sent()

    @pl.loop(0, 4)
    def _(f):
        fwd_of(f, core).wait_send()

    @pl.loop(0, 4)
    def _(i):
        f = (y + i) % 4
        up0f_of(f, 1 - core).wait_recv()

        subtract(pparent0, pparent0, pfront, pupper0.at[f], f * 4, 32, 4)

    @pl.loop(0, 8)
    def _(j):
        a = j + j // 4 * 4
        extend(pfront, pparent1, 1, a, a + 4)

    others(lambda to: pp1_of(r, to).start())

    @pl.loop(0, 8)
    def _(j):
        ppiv1[j, r] = pparent1[y // 2 * 8 + j, 0, 0:16, piece]

    open_stage(1, 0)
    open_stage(1, 1)
    open_stage(1, 2)

    others(lambda owner: pp1_of(owner, r).wait_recv())
    quarter = pl.ds(multiple(core * 256 + y % 2 * BLOCK, BLOCK), BLOCK)
    pupper1[y // 2, quarter, piece] = jnp.dot(
        inv[4 + y // 2, quarter, :], ppiv1[...].reshape(PANEL, BLOCK), preferred_element_type=F32
    ).astype(BF16)
    spread_upper1.begin()
    own_level1(0)
    spread_upper1.pass_on()
    own_level0(1)
    spread_upper1.take_direct()
    spread_upper1.take_passed()

    @pl.loop(0, 2)
    def _(f):
        up1f_of(f, core).start()

    @pl.loop(0, 2)
    def _(f):
        up1f_of(f, 1 - core).wait_recv()

        @pl.loop(0, 2)
        def _(j):
            subtract(pparent1, pparent1, pfront, pupper1.at[f], f * 8 + j * 4, 16, 4)

    @pl.loop(0, 8)
    def _(j):
        extend(pfront, pparent2, 2, j, j + 8)

    own_level2(0)
    own_level1(1)
    own_level2(1)

    for h in range(2):
        home(h).wait()

    def settle(dy, dx):
        slab = at(dy, dx)
        map_of(g, slab).wait_send()
        for h in range(2):
            out_of(h, slab, g).wait_recv()
            out_of(h, g, slab).wait_send()
            a2a_of(h, g, slab).wait_send()

    for stage in range(3):
        each_peer(stage, settle)
    spread_upper0.sent()
    spread_upper1.sent()

    @pl.loop(0, 4)
    def _(f):
        up0f_of(f, core).wait_send()

    @pl.loop(0, 2)
    def _(f):
        up1f_of(f, core).wait_send()

    def leave(to):
        pp0_of(r, to).wait_send()
        pp1_of(r, to).wait_send()
        for h in range(2):
            piv2_of(h, r, to).wait_send()

    others(leave)


def on_device(child_front, own_map, cross_map, pivot_inverse):
    rows, width = child_front.shape
    dma = pltpu.SemaphoreType.DMA
    call = pl.pallas_call(
        kernel,
        out_shape=jax.ShapeDtypeStruct((2, BLOCK, width), BF16),
        in_specs=[
            pl.BlockSpec(memory_space=pl.ANY),
            pl.BlockSpec(memory_space=pltpu.SMEM),
            pl.BlockSpec(memory_space=pltpu.SMEM),
            pl.BlockSpec(memory_space=pl.ANY),
        ],
        out_specs=pl.BlockSpec(memory_space=pl.ANY),
        scratch_shapes=[
            pltpu.VMEM((16, 2, BLOCK, HALF), BF16),
            pltpu.VMEM((16, 2, BLOCK, HALF), BF16),
            pltpu.VMEM((2, 16, 2, BLOCK, HALF), BF16),
            pltpu.VMEM((16, 2, BLOCK, PANEL), BF16),
            pltpu.VMEM((16, 2, BLOCK, PANEL), BF16),
            pltpu.VMEM((16, 2, BLOCK, PANEL), BF16),
            pltpu.VMEM((16, 2, BLOCK, PANEL), BF16),
            pltpu.VMEM((7, PANEL, PANEL), BF16),
            pltpu.VMEM((16, 8, 128), jnp.int32),
            pltpu.SMEM((16, 8, 128), jnp.int32),
            pltpu.VMEM((2, 16, 4, 32, HALF), BF16),
            pltpu.VMEM((2, 16, 4, 16, HALF), BF16),
            pltpu.VMEM((2, 4, 8, 16, HALF), BF16),
            pltpu.VMEM((16, 4, 8, HALF), F32),
            pltpu.VMEM((4, 4, 32, BLOCK), BF16),
            pltpu.VMEM((8, 4, 16, BLOCK), BF16),
            pltpu.VMEM((2, 4, PANEL, HALF), BF16),
            pltpu.VMEM((4, PANEL, PANEL), BF16),
            pltpu.VMEM((2, PANEL, PANEL), BF16),
            dma((16,)), dma((16,)), dma((2, 16)), dma((2, 16)), dma((3,)), dma((1,)),
            dma((4, 4)), dma((16,)), dma((4,)), dma((4,)), dma((2, 4, 4)), dma((2, 4, 4)),
            dma((2, 4)), dma((2, 4)), dma((2, 4)), dma((2, 4)), dma((4,)), dma((4,)),
            dma((4,)), dma((4,)), dma((4, 4)), dma((16,)), dma((4,)), dma((4,)),
            dma((4, 4)), dma((16,)), dma((2,)), dma((2,)), dma((2, 16)), dma((2, 16)), dma((6,)),
        ],
        compiler_params=pltpu.CompilerParams(
            collective_id=0, has_side_effects=True, vmem_limit_bytes=60 * 1024 * 1024
        ),
        cost_estimate=pl.CostEstimate(
            flops=9_000_000_000, bytes_accessed=16_000_000, transcendentals=0
        ),
    )
    tables = [table[:, 0, :].T for table in (own_map, cross_map)]
    result = call(child_front.reshape(2, BLOCK, width), *tables, pivot_inverse)
    return result.reshape(rows, width)


def solution(mesh):
    placed = (P("leaf", "panel"), P(None, "leaf", None), P(None, "leaf", None), P())
    return jax.shard_map(
        on_device, mesh=mesh, in_specs=placed, out_specs=P("leaf", "panel"), check_vma=False
    )
```

```python
import functools

import jax
import jax.numpy as jnp
from jax import lax
from jax.experimental import pallas as pl
from jax.experimental.pallas import tpu as pltpu
from jax.sharding import PartitionSpec as P

PANEL = 512
BLOCK = 128
WIDTH = 256
HALF = 128
MESH = pl.DeviceIdType.MESH
F32 = jnp.float32
BF16 = jnp.bfloat16


def multiple(value, of):
    return pl.multiple_of(value, of)


def kernel(
    child, own_map, cross_map, inverse, out,
    front_a, front_b, parent, pfront, pparent0, pparent1, pparent2, inv, map_buf, map_tab,
    piv0, piv1, piv2, piv2_wide, ppiv0, ppiv1, upper, pupper0, pupper1,
    map_send, map_recv, a2a_send, a2a_recv, first_send, first_recv,
    pan_send, pan_recv, fwd_send, fwd_recv, piv0_send, piv0_recv,
    piv1_send, piv1_recv, piv2_send, piv2_recv, pp0_send, pp0_recv,
    pp1_send, pp1_recv, up0_send, up0_recv, up0f_send, up0f_recv,
    up1_send, up1_recv, up1f_send, up1f_recv, out_send, out_recv, local_sem,
):
    fronts = (front_a, front_b)
    leaf = lax.axis_index("leaf")
    panel = lax.axis_index("panel")
    g, r = leaf // 4, leaf % 4
    y, x = g // 4, g % 4
    core = panel % 2
    mate = panel + 1 - 2 * core

    def at(dy, dx):
        return ((y + dy) % 4) * 4 + (x + dx) % 4

    def each_peer(stage, visit):
        if stage == 0:
            @pl.loop(1, 4)
            def _(i):
                visit(0, i)
        elif stage == 1:
            @pl.loop(0, 4)
            def _(i):
                visit(1, i)
                visit(3, i)
        else:
            @pl.loop(0, 4)
            def _(i):
                visit(2, i)

    def remote(src, dst, send, recv, to_leaf, to_panel):
        return pltpu.make_async_remote_copy(
            src_ref=src, dst_ref=dst, send_sem=send, recv_sem=recv,
            device_id=(to_leaf, to_panel), device_id_type=MESH,
        )

    def crossed(first, second):
        return at(core * first + (1 - core) * second, core * second + (1 - core) * first)

    class Spread:
        def __init__(self, part_of, send, recv):
            self.part_of, self.send, self.recv = part_of, send, recv

        def copy(self, slab, i, j, to):
            part = self.part_of(slab)
            return remote(part, part, self.send.at[i, j], self.recv.at[slab], to * 4 + r, panel)

        def begin(self):
            @pl.loop(1, 4)
            def _(i):
                self.copy(g, i, 0, crossed(i, 0)).start()
                self.copy(g, 0, i, crossed(0, i)).start()

        def pass_on(self):
            @pl.loop(1, 4)
            def _(i):
                slab = crossed(i, 0)
                self.copy(slab, 0, 0, g).wait_recv()

                @pl.loop(1, 4)
                def _(j):
                    self.copy(slab, i, j, crossed(0, j)).start()

        def take_direct(self):
            @pl.loop(1, 4)
            def _(j):
                self.copy(crossed(0, j), 0, 0, g).wait_recv()

        def take_row(self, dy):
            @pl.loop(1, 4)
            def _(i):
                self.copy(at(dy, i), 0, 0, g).wait_recv()

        def take_passed(self):
            @pl.loop(1, 4)
            def _(i):
                @pl.loop(1, 4)
                def _(j):
                    self.copy(crossed(i, j), 0, 0, g).wait_recv()

        def sent(self):
            @pl.loop(1, 4)
            def _(i):
                self.copy(g, i, 0, crossed(i, 0)).wait_send()
                self.copy(g, 0, i, crossed(0, i)).wait_send()

                @pl.loop(1, 4)
                def _(j):
                    self.copy(crossed(i, 0), i, j, crossed(0, j)).wait_send()

    barrier = pltpu.get_barrier_semaphore()

    def greet(dy, dx):
        pl.semaphore_signal(barrier, inc=1, device_id=(at(dy, dx) * 4 + r, panel), device_id_type=MESH)

    @pl.loop(1, 4)
    def _(i):
        pl.semaphore_signal(barrier, inc=1, device_id=(leaf, (panel + i) % 4), device_id_type=MESH)

    for stage in (2, 1, 0):
        each_peer(stage, greet)

    @pl.loop(1, 4)
    def _(i):
        pl.semaphore_signal(barrier, inc=1, device_id=(g * 4 + (r + i) % 4, panel), device_id_type=MESH)

    def columns(which, h):
        return pl.ds(multiple(which * WIDTH + h * HALF, HALF), HALF)

    def own_copy(h):
        return pltpu.make_async_copy(child.at[:, :, columns(g, h)], fronts[h].at[g], local_sem.at[4 + h])

    own_copy(0).start()
    own_copy(1).start()
    inv_copy = pltpu.make_async_copy(inverse, inv, local_sem.at[1])
    inv_copy.start()
    row = lax.broadcasted_iota(jnp.int32, (8, 128), 0)
    lane = lax.broadcasted_iota(jnp.int32, (8, 128), 1)
    table = jnp.zeros((8, 128), jnp.int32)
    for level in range(3):
        for slot in range(2):
            table = jnp.where((row == level) & (lane == slot), own_map[slot, level], table)
            table = jnp.where((row == level) & (lane == 2 + slot), cross_map[slot, level], table)
    map_buf[g] = table
    pl.semaphore_wait(barrier, 21)

    def first_copy(half, to_panel, index):
        return remote(
            child.at[half, :, pl.ds(0, PANEL)], pfront.at[g, half],
            first_send.at[index], first_recv.at[0], leaf, to_panel,
        )

    first_own = pltpu.make_async_copy(child.at[0, :, pl.ds(0, PANEL)], pfront.at[g, 0], local_sem.at[3])

    @pl.when(panel == 0)
    def _():
        first_copy(0, 2, 1).start()
        first_copy(1, 3, 2).start()
        first_copy(1, 1, 0).start()
        first_own.start()

    def map_of(slab, to):
        return remote(map_buf.at[slab], map_buf.at[slab], map_send.at[to], map_recv.at[slab], to * 4 + r, panel)

    def a2a_of(h, slab, to):
        return remote(
            child.at[:, :, columns(to, h)], fronts[h].at[slab],
            a2a_send.at[h, to], a2a_recv.at[h, slab], to * 4 + r, panel,
        )

    spread_panel = Spread(lambda slab: pfront.at[slab, core], pan_send, pan_recv)

    def send_child(h, stage):
        each_peer(stage, lambda dy, dx: a2a_of(h, g, at(dy, dx)).start())

    for stage in range(3):
        each_peer(stage, lambda dy, dx: map_of(g, at(dy, dx)).start())
    for stage in range(3):
        send_child(0, stage)

    @pl.when(panel == 0)
    def _():
        first_own.wait()

    @pl.when(panel != 0)
    def _():
        first_copy(core, panel, 0).wait_recv()

    spread_panel.begin()


    def take_map(dy, dx):
        map_of(at(dy, dx), g).wait_recv()

    for stage in range(3):
        each_peer(stage, take_map)
    to_smem = pltpu.make_async_copy(map_buf, map_tab, local_sem.at[2])
    to_smem.start()
    to_smem.wait()

    def extend(src, dst, level, a, b):
        width = src.shape[3]
        step = min(width, WIDTH)
        for mine, other in ((a, b), (b, a)):
            for slot in range(2):
                own_block = map_tab[mine, level, slot]
                cross_block = map_tab[mine, level, 2 + slot]

                @pl.loop(0, BLOCK // 32)
                def _(q):
                    for left in range(0, width, step):
                        part = (pl.ds(multiple(q * 32, 32), 32), pl.ds(left, step))
                        if level:
                            kept, moved = src[(mine, own_block) + part], src[(other, cross_block) + part]
                        else:
                            kept = jnp.where(own_block == 0, src[(mine, 0) + part], src[(mine, 1) + part])
                            moved = jnp.where(cross_block == 0, src[(other, 0) + part], src[(other, 1) + part])
                        dst[(mine, slot) + part] = (kept.astype(F32) + moved.astype(F32)).astype(BF16)

    def subtract(src, columns_of, dst, factor, slab, rows, count=2):
        width = src.shape[3]
        step = min(width, WIDTH)
        slabs = pl.ds(slab, count)
        left = columns_of[slabs].reshape(count * 2 * BLOCK, PANEL)
        for low in range(0, width, step):
            part = pl.ds(low, step)
            product = jnp.dot(left, factor[:, part], preferred_element_type=F32)
            start = src[slabs, :, :, part].reshape(count * 2 * BLOCK, step).astype(F32)
            dst[slabs, :, :, part] = (start - product).astype(BF16).reshape(count, 2, BLOCK, step)
        for k in range(count):
            if rows % 16:
                keep = lax.broadcasted_iota(jnp.int32, (16, width), 0) >= rows
                top = dst[slab + k, 0, 0:16, :].astype(F32)
                dst[slab + k, 0, 0:16, :] = jnp.where(keep, top, 0.0).astype(BF16)
            else:
                dst[slab + k, 0, 0:rows, :] = jnp.zeros((rows, width), BF16)

    def piv0_of(h, f, owner, to):
        slabs = pl.ds(f * 4, 4)
        return remote(
            parent.at[h, slabs, 0, pl.ds(0, 32), :], piv0.at[h, slabs, owner],
            piv0_send.at[h, f, to], piv0_recv.at[h, f, owner], g * 4 + to, panel,
        )

    def fwd_of(f, half):
        part = pfront.at[pl.ds(f * 4, 4), half]
        return remote(part, part, fwd_send.at[f], fwd_recv.at[f], leaf, mate)

    def open_front(h, f):
        @pl.loop(0, 2)
        def _(j):
            extend(fronts[h], parent.at[h], 0, f * 4 + j, f * 4 + j + 2)

        @pl.loop(1, 4)
        def _(i):
            piv0_of(h, f, r, (r + i) % 4).start()

        @pl.loop(0, 4)
        def _(j):
            piv0[h, f * 4 + j, r] = parent[h, f * 4 + j, 0, 0:32, :]

    def open_stage(h, stage):
        each_peer(stage, lambda dy, dx: a2a_of(h, at(dy, dx), g).wait_recv())
        if stage == 0:
            own_copy(h).wait()
            open_front(h, y)
        elif stage == 1:
            @pl.loop(0, 2)
            def _(i):
                open_front(h, (y + 1 + 2 * i) % 4)
        else:
            open_front(h, (y + 2) % 4)

    def open_panel(f):
        fwd_of(f, 1 - core).wait_recv()

        @pl.loop(0, 2)
        def _(j):
            extend(pfront, pparent0, 0, f * 4 + j, f * 4 + j + 2)

    piece = pl.ds(multiple(x * BLOCK, BLOCK), BLOCK)

    def pp0_of(owner, to):
        return remote(
            pparent0.at[pl.ds(y * 4, 4), 0, pl.ds(0, 32), piece], ppiv0.at[:, owner],
            pp0_send.at[to], pp0_recv.at[owner], g * 4 + to, panel,
        )

    spread_upper0 = Spread(
        lambda slab: pupper0.at[
            slab // 4, pl.ds(multiple(core * 256, 256), 256), pl.ds(multiple(slab % 4 * BLOCK, BLOCK), BLOCK)
        ],
        up0_send, up0_recv,
    )

    def up0f_of(f, half):
        part = pupper0.at[f, pl.ds(multiple(half * 256, 256), 256), :]
        return remote(part, part, up0f_send.at[f], up0f_recv.at[f], leaf, mate)

    def piv1_of(h, owner, to):
        return remote(
            parent.at[h, :, 0, pl.ds(0, 16), :], piv1.at[h, :, owner],
            piv1_send.at[h, to], piv1_recv.at[h, owner], g * 4 + to, panel,
        )

    def pp1_of(owner, to):
        return remote(
            pparent1.at[pl.ds(y // 2 * 8, 8), 0, pl.ds(0, 16), piece], ppiv1.at[:, owner],
            pp1_send.at[to], pp1_recv.at[owner], g * 4 + to, panel,
        )

    spread_upper1 = Spread(
        lambda slab: pupper1.at[
            slab // 8,
            pl.ds(multiple(core * 256 + slab // 4 % 2 * BLOCK, BLOCK), BLOCK),
            pl.ds(multiple(slab % 4 * BLOCK, BLOCK), BLOCK),
        ],
        up1_send, up1_recv,
    )

    def up1f_of(f, half):
        part = pupper1.at[f, pl.ds(multiple(half * 256, 256), 256), :]
        return remote(part, part, up1f_send.at[f], up1f_recv.at[f], leaf, mate)

    def piv2_of(h, owner, to):
        part = piv2.at[h, owner]
        return remote(part, part, piv2_send.at[h, to], piv2_recv.at[h, owner], g * 4 + to, panel)

    def out_of(h, slab, to):
        return remote(
            fronts[h].at[to], out.at[:, :, columns(slab, h)],
            out_send.at[h, to], out_recv.at[h, slab], to * 4 + r, panel,
        )

    def others(visit):
        @pl.loop(1, 4)
        def _(i):
            visit((r + i) % 4)

    def own_level0(h):
        @pl.loop(0, 4)
        def _(i):
            f = (y + i + i // 2 - 2 * (i // 3)) % 4
            others(lambda owner: piv0_of(h, f, owner, r).wait_recv())
            upper[h, f] = jnp.dot(
                inv[f], piv0[h, pl.ds(f * 4, 4)].reshape(PANEL, HALF), preferred_element_type=F32
            ).astype(BF16)

            subtract(parent.at[h], pparent0, fronts[h], upper.at[h, f], f * 4, 32, 4)

        @pl.loop(0, 4)
        def _(f):
            others(lambda to: piv0_of(h, f, r, to).wait_send())

        @pl.loop(0, 8)
        def _(j):
            a = j + j // 4 * 4
            extend(fronts[h], parent.at[h], 1, a, a + 4)

        others(lambda to: piv1_of(h, r, to).start())

        @pl.loop(0, 16)
        def _(j):
            piv1[h, j, r] = parent[h, j, 0, 0:16, :]

    def own_level1(h):
        others(lambda owner: piv1_of(h, owner, r).wait_recv())

        @pl.loop(0, 2)
        def _(f):
            upper[h, f] = jnp.dot(
                inv[4 + f], piv1[h, pl.ds(f * 8, 8)].reshape(PANEL, HALF), preferred_element_type=F32
            ).astype(BF16)

            @pl.loop(0, 2)
            def _(j):
                subtract(parent.at[h], pparent1, fronts[h], upper.at[h, f], f * 8 + j * 4, 16, 4)

        others(lambda to: piv1_of(h, r, to).wait_send())

        @pl.loop(0, 8)
        def _(j):
            extend(fronts[h], parent.at[h], 2, j, j + 8)

        @pl.loop(0, 8)
        def _(j):
            pair = [parent[h, 2 * j + k, 0, 0:16, :].astype(F32)[0:8] for k in range(2)]
            piv2[h, r, j] = jnp.concatenate(pair, axis=0).astype(BF16)

        others(lambda to: piv2_of(h, r, to).start())

    def own_level2(h):
        others(lambda owner: piv2_of(h, owner, r).wait_recv())

        @pl.loop(0, 4)
        def _(owner):
            @pl.loop(0, 8)
            def _(j):
                both = piv2[h, owner, j].astype(F32)
                piv2_wide[2 * j, owner] = both[0:8]
                piv2_wide[2 * j + 1, owner] = both[8:16]

        upper[h, 0] = jnp.dot(
            inv[6], piv2_wide[...].reshape(PANEL, HALF).astype(BF16), preferred_element_type=F32
        ).astype(BF16)

        def finish(dy, dx):
            to = at(dy, dx)
            subtract(parent.at[h], pparent2, fronts[h], upper.at[h, 0], to, 8, 1)
            out_of(h, g, to).start()

        for stage in range(3):
            each_peer(stage, finish)
        subtract(parent.at[h], pparent2, fronts[h], upper.at[h, 0], g, 8, 1)
        home(h).start()

    def home(h):
        return pltpu.make_async_copy(fronts[h].at[g], out.at[:, :, columns(g, h)], local_sem.at[4 + h])

    for stage in range(3):
        open_stage(0, stage)
    spread_panel.pass_on()
    send_child(1, 0)
    spread_panel.take_direct()
    fwd_of(y, core).start()
    open_panel(y)
    others(lambda to: pp0_of(r, to).start())

    @pl.loop(0, 4)
    def _(j):
        ppiv0[j, r] = pparent0[y * 4 + j, 0, 0:32, piece]

    send_child(1, 1)
    inv_copy.wait()
    others(lambda owner: pp0_of(owner, r).wait_recv())
    half0 = pl.ds(multiple(core * 256, 256), 256)
    pupper0[y, half0, piece] = jnp.dot(
        inv[y, half0, :], ppiv0[...].reshape(PANEL, BLOCK), preferred_element_type=F32
    ).astype(BF16)
    spread_upper0.begin()

    @pl.loop(1, 4)
    def _(i):
        spread_panel.take_row(i)
        fwd_of((y + i) % 4, core).start()

    spread_upper0.pass_on()
    send_child(1, 2)

    @pl.loop(1, 4)
    def _(i):
        open_panel((y + i) % 4)

    own_level0(0)
    open_stage(1, 0)
    open_stage(1, 1)

    spread_upper0.take_direct()
    up0f_of(y, core).start()

    @pl.loop(1, 4)
    def _(i):
        spread_upper0.take_row(i)
        up0f_of((y + i) % 4, core).start()

    @pl.when(panel == 0)
    def _():
        for index in range(3):
            first_copy(0, 1, index).wait_send()

    spread_panel.sent()

    @pl.loop(0, 4)
    def _(f):
        fwd_of(f, core).wait_send()

    @pl.loop(0, 4)
    def _(i):
        f = (y + i) % 4
        up0f_of(f, 1 - core).wait_recv()

        subtract(pparent0, pparent0, pfront, pupper0.at[f], f * 4, 32, 4)

    @pl.loop(0, 8)
    def _(j):
        a = j + j // 4 * 4
        extend(pfront, pparent1, 1, a, a + 4)

    others(lambda to: pp1_of(r, to).start())

    @pl.loop(0, 8)
    def _(j):
        ppiv1[j, r] = pparent1[y // 2 * 8 + j, 0, 0:16, piece]

    open_stage(1, 2)
    own_level1(0)

    others(lambda owner: pp1_of(owner, r).wait_recv())
    quarter = pl.ds(multiple(core * 256 + y % 2 * BLOCK, BLOCK), BLOCK)
    pupper1[y // 2, quarter, piece] = jnp.dot(
        inv[4 + y // 2, quarter, :], ppiv1[...].reshape(PANEL, BLOCK), preferred_element_type=F32
    ).astype(BF16)
    spread_upper1.begin()
    spread_upper1.pass_on()
    own_level0(1)
    spread_upper1.take_direct()
    spread_upper1.take_passed()

    @pl.loop(0, 2)
    def _(f):
        up1f_of(f, core).start()

    @pl.loop(0, 2)
    def _(f):
        up1f_of(f, 1 - core).wait_recv()

        @pl.loop(0, 2)
        def _(j):
            subtract(pparent1, pparent1, pfront, pupper1.at[f], f * 8 + j * 4, 16, 4)

    @pl.loop(0, 8)
    def _(j):
        extend(pfront, pparent2, 2, j, j + 8)

    own_level2(0)
    own_level1(1)
    own_level2(1)

    for h in range(2):
        home(h).wait()

    def settle(dy, dx):
        slab = at(dy, dx)
        map_of(g, slab).wait_send()
        for h in range(2):
            out_of(h, slab, g).wait_recv()
            out_of(h, g, slab).wait_send()
            a2a_of(h, g, slab).wait_send()

    for stage in range(3):
        each_peer(stage, settle)
    spread_upper0.sent()
    spread_upper1.sent()

    @pl.loop(0, 4)
    def _(f):
        up0f_of(f, core).wait_send()

    @pl.loop(0, 2)
    def _(f):
        up1f_of(f, core).wait_send()

    def leave(to):
        pp0_of(r, to).wait_send()
        pp1_of(r, to).wait_send()
        for h in range(2):
            piv2_of(h, r, to).wait_send()

    others(leave)


def on_device(child_front, own_map, cross_map, pivot_inverse):
    rows, width = child_front.shape
    dma = pltpu.SemaphoreType.DMA
    call = pl.pallas_call(
        kernel,
        out_shape=jax.ShapeDtypeStruct((2, BLOCK, width), BF16),
        in_specs=[
            pl.BlockSpec(memory_space=pl.ANY),
            pl.BlockSpec(memory_space=pltpu.SMEM),
            pl.BlockSpec(memory_space=pltpu.SMEM),
            pl.BlockSpec(memory_space=pl.ANY),
        ],
        out_specs=pl.BlockSpec(memory_space=pl.ANY),
        scratch_shapes=[
            pltpu.VMEM((16, 2, BLOCK, HALF), BF16),
            pltpu.VMEM((16, 2, BLOCK, HALF), BF16),
            pltpu.VMEM((2, 16, 2, BLOCK, HALF), BF16),
            pltpu.VMEM((16, 2, BLOCK, PANEL), BF16),
            pltpu.VMEM((16, 2, BLOCK, PANEL), BF16),
            pltpu.VMEM((16, 2, BLOCK, PANEL), BF16),
            pltpu.VMEM((16, 2, BLOCK, PANEL), BF16),
            pltpu.VMEM((7, PANEL, PANEL), BF16),
            pltpu.VMEM((16, 8, 128), jnp.int32),
            pltpu.SMEM((16, 8, 128), jnp.int32),
            pltpu.VMEM((2, 16, 4, 32, HALF), BF16),
            pltpu.VMEM((2, 16, 4, 16, HALF), BF16),
            pltpu.VMEM((2, 4, 8, 16, HALF), BF16),
            pltpu.VMEM((16, 4, 8, HALF), F32),
            pltpu.VMEM((4, 4, 32, BLOCK), BF16),
            pltpu.VMEM((8, 4, 16, BLOCK), BF16),
            pltpu.VMEM((2, 4, PANEL, HALF), BF16),
            pltpu.VMEM((4, PANEL, PANEL), BF16),
            pltpu.VMEM((2, PANEL, PANEL), BF16),
            dma((16,)), dma((16,)), dma((2, 16)), dma((2, 16)), dma((3,)), dma((1,)),
            dma((4, 4)), dma((16,)), dma((4,)), dma((4,)), dma((2, 4, 4)), dma((2, 4, 4)),
            dma((2, 4)), dma((2, 4)), dma((2, 4)), dma((2, 4)), dma((4,)), dma((4,)),
            dma((4,)), dma((4,)), dma((4, 4)), dma((16,)), dma((4,)), dma((4,)),
            dma((4, 4)), dma((16,)), dma((2,)), dma((2,)), dma((2, 16)), dma((2, 16)), dma((6,)),
        ],
        compiler_params=pltpu.CompilerParams(
            collective_id=0, has_side_effects=True, vmem_limit_bytes=60 * 1024 * 1024
        ),
        cost_estimate=pl.CostEstimate(
            flops=9_000_000_000, bytes_accessed=16_000_000, transcendentals=0
        ),
    )
    tables = [table[:, 0, :].T for table in (own_map, cross_map)]
    result = call(child_front.reshape(2, BLOCK, width), *tables, pivot_inverse)
    return result.reshape(rows, width)


def solution(mesh):
    placed = (P("leaf", "panel"), P(None, "leaf", None), P(None, "leaf", None), P())
    return jax.shard_map(
        on_device, mesh=mesh, in_specs=placed, out_specs=P("leaf", "panel"), check_vma=False
    )
```
